32 devices in a mesh: mem: 4 (over y, x), lat: 8 (over z, core).
Axes of the slice: x: 2, y: 2, z: 4, core: 2. Of those that a mesh axis runs over, the one named last changes fastest.
Arguments:
- prior_member_stack: float32 [64, 16, 64, 512], P('mem', None, 'lat'), may hold values from -6 to 6
- zonal_stability_ratio: float32 [64, 512], P('lat'), may hold values from -0.45 to 0.45
- meridional_stability_ratio: float32 [64, 512], P('lat'), may hold values from -0.45 to 0.45
- obs_perturb: bfloat16 [512, 64, 4096], P(('mem', 'lat')), may hold values from -2 to 2
- innovation: float32 [512, 4096], P(('mem', 'lat')), may hold values from -6 to 6
- inverse_error_variance: float32 [512, 4096], P(('mem', 'lat')), may hold values from 0.25 to 4
- obs_count: int32 [512], P(('mem', 'lat')), may hold values from 1 to 4096, 1048576 in all
- neighbours: int32 [512, 6], P(('mem', 'lat')), may hold values from 0 to 47, as said below
- localization: float32 [512, 6], P(('mem', 'lat')), may hold values from 0.2 to 1
Outputs:
- analysis: float32 [64, 16, 512, 64], P(None, None, ('mem', 'lat'))
The draws below stay inside these ranges and needn't reach their ends.
Inputs may be any that keep to these rules, and one draw needn't show every extreme that they name: The observations of a tile fill its first obs_count slots; later slots are ignored. `neighbours`: window index w names row group w % 16 of the strip w // 16 - 1 places east (strips wrap around). Entry 0 of each row is the tile itself; the others are distinct tiles of the previous, same or next row group in the previous, same or next strip.
All inputs are finite; a program needn't handle non-finite values. No bound on the sum of `obs_count` on one device may be relied on, other than what follows from the above.
Results may differ from the reference program's by a relative error of at most 0.0022.
Values may be sent and summed in bfloat16 or wider, within the bound.
A program may use at most 256 MiB of HBM per device.

```python
import math
import jax
import jax.numpy as jnp
import numpy as np
from jax import lax

ENSEMBLE_SIZE = 64
CH = 16
NLON = 512
TILES_DEV = 16
OBS_CAP = 4096
NEIGH = 6
NS_ITERS = 5
NLAT = 64
TILES = 512
TILE_ROWS = 4
LON_DEV = 16
DEVICES = 32


def draw_neighbours(key, part):
    key = jax.random.fold_in(key, 7)
    latitude_row_group = jnp.arange(TILES, dtype=jnp.int32) % TILES_DEV
    offsets = jnp.arange(9, dtype=jnp.int32)
    strip_step = offsets // 3 - 1
    row_step = offsets % 3 - 1
    destination_parallel = latitude_row_group[:, None] + row_step[None, :]
    inside = (destination_parallel >= 0) & (destination_parallel < TILES_DEV) & (offsets[None, :] != 4)
    scores = jax.random.randint(key, (TILES, 9), 0, 1 << 20, dtype=jnp.int32) * 16 + offsets[None, :]
    scores = jnp.where(inside, scores, -1)
    picked = lax.top_k(scores, NEIGH - 1)[1].astype(jnp.int32)
    window_index = (strip_step[picked] + 1) * TILES_DEV + latitude_row_group[:, None] + row_step[picked]
    self_index = TILES_DEV + latitude_row_group
    return jnp.concatenate([self_index[:, None], window_index], axis=1).astype(jnp.int32)


def level_of(rng, shape, shards, least, largest):
    def one(position, shards_of):
        heights = jax.random.uniform(jax.random.fold_in(jax.random.fold_in(rng, 6), position), (shards_of,), jnp.float32, least / len(shards), largest / len(shards))
        return jnp.repeat(jnp.exp(heights), shape[position] // shards_of).reshape((-1,) + (1,) * (len(shape) - position - 1))

    level = one(*shards[0])
    for cut in shards[1:]:
        level = level * one(*cut)
    return level


def profile(number_of, total, limit, skew):
    weights = [(1 << 20) // math.isqrt(standing ** skew) + 1 for standing in range(2, number_of + 1)]
    rest, given = total - limit - (number_of - 1), [1] * (number_of - 1)
    while rest > 0:
        movable = [i for i in range(number_of - 1) if given[i] < limit]
        pool, remaining = sum([weights[i] for i in movable]), rest
        for i in movable:
            more = min(limit - given[i], max(1, remaining * weights[i] // pool), rest)
            given[i] = given[i] + more
            rest = rest - more
    return np.array([limit] + given)


def ragged(key, count, total, reach, lean):
    if count == 2:
        one = jax.random.randint(key, (), max(1, total - reach), min(reach, total - 1) + 1)
        return jnp.stack([one, total - one])
    lengths = jnp.asarray(profile(count, total, reach, lean), jnp.int32)
    twos = (count - 1) // 2
    giver, sink = lengths[1:1 + 2 * twos:2], lengths[2:2 + 2 * twos:2]
    room = jnp.minimum(giver - 1, reach - sink)
    moved = jax.random.randint(jax.random.fold_in(key, 1), (twos,), 0, 1 << 20) % (room + 1)
    lengths = lengths.at[1:1 + 2 * twos:2].set(giver - moved).at[2:2 + 2 * twos:2].set(sink + moved)
    return lengths[jax.random.permutation(jax.random.fold_in(key, 2), count)]


def bell_draw(stream_key, extent, width, reach, pieces=(), held_as=jnp.bfloat16):
    gain = level_of(stream_key, extent, pieces, -0.22, 0.18) if pieces else 1.0
    array = jax.random.normal(stream_key, extent, jnp.float32) * width * gain
    return jnp.minimum(jnp.maximum(array, -reach), reach).astype(held_as)


def setup_inputs(seed: int = 0) -> dict:
    seeds = jax.random.split(jax.random.key(seed), 10)
    return {
        "prior_member_stack": bell_draw(seeds[0], (ENSEMBLE_SIZE, CH, NLAT, NLON), 1.0, 6.0, ((0, 4), (2, 8)), jnp.float32),
        "zonal_stability_ratio": jnp.clip(jax.random.uniform(seeds[1], (NLAT, NLON), jnp.float32, -0.45, 0.45) * level_of(seeds[1], (NLAT, NLON), ((0, 8),), -0.4, 0.0), -0.45, 0.45),
        "meridional_stability_ratio": jnp.clip(jax.random.uniform(seeds[2], (NLAT, NLON), jnp.float32, -0.45, 0.45) * level_of(seeds[2], (NLAT, NLON), ((0, 8),), -0.4, 0.0), -0.45, 0.45),
        "obs_perturb": bell_draw(seeds[3], (TILES, ENSEMBLE_SIZE, OBS_CAP), 0.3, 2.0, ((0, 32),)),
        "innovation": bell_draw(seeds[4], (TILES, OBS_CAP), 1.0, 6.0, ((0, 32),), jnp.float32),
        "inverse_error_variance": jnp.clip(jnp.exp(math.log(4.0) - 2.7725887 * jax.random.uniform(seeds[5], (TILES, OBS_CAP), jnp.float32) ** level_of(seeds[5], (TILES, OBS_CAP), ((0, 32),), -0.2, 0.2)), 0.25, 4.0),
        "obs_count": ragged(seeds[6], TILES, TILES * OBS_CAP // 2, OBS_CAP, 2).astype(jnp.int32),
        "neighbours": draw_neighbours(jax.random.fold_in(seeds[9], 71), 0),
        "localization": jnp.clip(jnp.exp(math.log(1.0) - 1.609438 * jax.random.uniform(seeds[8], (TILES, NEIGH), jnp.float32) ** level_of(seeds[8], (TILES, NEIGH), ((0, 32),), -0.2, 0.2)), 0.2, 1.0),
    }


def predict_model_state(prior_member_stack, zonal_stability_ratio, meridional_stability_ratio):
    east_neighbour = jnp.roll(prior_member_stack, -1, axis=-1)
    eastward_flux = jnp.maximum(zonal_stability_ratio, 0.0) * prior_member_stack + jnp.minimum(zonal_stability_ratio, 0.0) * east_neighbour
    divergence_x = eastward_flux - jnp.roll(eastward_flux, 1, axis=-1)
    zero_row = jnp.zeros(prior_member_stack.shape[:2] + (1, prior_member_stack.shape[3]), jnp.float32)
    fields_ext = jnp.concatenate([zero_row, prior_member_stack, zero_row], axis=2)
    north_ext = jnp.concatenate([jnp.zeros((1, meridional_stability_ratio.shape[1]), jnp.float32), meridional_stability_ratio], axis=0)
    flux_north = jnp.maximum(north_ext, 0.0) * fields_ext[:, :, :-1] + jnp.minimum(north_ext, 0.0) * fields_ext[:, :, 1:]
    return prior_member_stack - divergence_x - (flux_north[:, :, 1:] - flux_north[:, :, :-1])

def tile_terms(arrays):
    perturb, weight, drive = arrays
    weighted = (perturb.astype(jnp.float32) * weight.astype(jnp.float32)[:, None, :]).astype(jnp.bfloat16)
    gram_matrix = jnp.einsum('tko,tlo->tkl', weighted.astype(jnp.float32), perturb.astype(jnp.float32), precision=lax.Precision.HIGHEST)
    drive_vector = jnp.einsum('tko,to->tk', perturb.astype(jnp.float32), drive.astype(jnp.float32), precision=lax.Precision.HIGHEST)
    return (gram_matrix, drive_vector)

def transform_weights(curvature, drive_total, members):
    frob_scale = jnp.sqrt(lax.optimization_barrier(jnp.sum(curvature * curvature, axis=(1, 2))))
    identity = jnp.eye(members, dtype=jnp.float32)[None]
    current = curvature / frob_scale[:, None, None]
    inverse = jnp.broadcast_to(identity, curvature.shape)
    for _ in range(NS_ITERS):
        middle = 1.5 * identity - 0.5 * jnp.einsum('tij,tjk->tik', inverse, current, precision=lax.Precision.HIGHEST)
        current = jnp.einsum('tij,tjk->tik', current, middle, precision=lax.Precision.HIGHEST)
        inverse = jnp.einsum('tij,tjk->tik', middle, inverse, precision=lax.Precision.HIGHEST)
    spread_part = jnp.sqrt((members - 1.0) / frob_scale)[:, None, None] * inverse
    half_step = jnp.einsum('tij,tj->ti', inverse, drive_total, precision=lax.Precision.HIGHEST)
    ensemble_mean_portion = jnp.einsum('tij,tj->ti', inverse, half_step, precision=lax.Precision.HIGHEST) / frob_scale[:, None]
    return spread_part + ensemble_mean_portion[:, :, None]

def reference(prior_member_stack, zonal_stability_ratio, meridional_stability_ratio, obs_perturb, innovation, inverse_error_variance, obs_count, neighbours, localization):
    transported_quantities = predict_model_state(prior_member_stack, zonal_stability_ratio, meridional_stability_ratio)
    is_valid = jnp.arange(OBS_CAP, dtype=jnp.int32)[None, :] < obs_count[:, None]
    obs_weight = jnp.where(is_valid, inverse_error_variance, 0.0).astype(jnp.bfloat16)
    obs_drive = jnp.where(is_valid, inverse_error_variance * innovation, 0.0).astype(jnp.bfloat16)
    gram_matrix, drive_vector = lax.map(tile_terms, (obs_perturb.reshape(DEVICES, TILES_DEV, ENSEMBLE_SIZE, OBS_CAP), obs_weight.reshape(DEVICES, TILES_DEV, OBS_CAP), obs_drive.reshape(DEVICES, TILES_DEV, OBS_CAP)))
    gram_matrix = gram_matrix.reshape(TILES, ENSEMBLE_SIZE, ENSEMBLE_SIZE)
    drive_vector = drive_vector.reshape(TILES, ENSEMBLE_SIZE)
    strip_of = jnp.arange(TILES, dtype=jnp.int32) // TILES_DEV
    sources = (strip_of[:, None] + neighbours // TILES_DEV - 1) % DEVICES * TILES_DEV + neighbours % TILES_DEV
    sources = sources.astype(jnp.int32)
    curvature = jnp.broadcast_to((ENSEMBLE_SIZE - 1.0) * jnp.eye(ENSEMBLE_SIZE, dtype=jnp.float32), (TILES, ENSEMBLE_SIZE, ENSEMBLE_SIZE))
    drive_total = jnp.zeros((TILES, ENSEMBLE_SIZE), jnp.float32)
    for slot_index in range(NEIGH):
        curvature = curvature + localization[:, slot_index, None, None] * gram_matrix[sources[:, slot_index]]
        drive_total = drive_total + localization[:, slot_index, None] * drive_vector[sources[:, slot_index]]
    weights = transform_weights(curvature, drive_total, ENSEMBLE_SIZE)
    grid = jnp.transpose(transported_quantities, (0, 1, 3, 2)).reshape(ENSEMBLE_SIZE, CH, DEVICES, LON_DEV, TILES_DEV, TILE_ROWS)
    member_mean = lax.optimization_barrier(jnp.mean(grid, axis=0))
    anomaly = grid - member_mean
    update = jnp.einsum('icsxtr,stij->jcsxtr', anomaly, weights.reshape(DEVICES, TILES_DEV, ENSEMBLE_SIZE, ENSEMBLE_SIZE), precision=lax.Precision.HIGHEST)
    return (member_mean + update).reshape(ENSEMBLE_SIZE, CH, NLON, NLAT)
```

```python
import jax
import jax.numpy as jnp
from jax import lax
from jax.experimental import pallas as pl
from jax.experimental.pallas import tpu as pltpu
from jax.sharding import PartitionSpec as P

NS_ITERS = 5
VMEM_BYTES = 48 * 1024 * 1024


def extended(x, sides, width, wrap):
    for axis, dim in sides:
        size, length = (lax.axis_size(axis), x.shape[dim])
        up = [(i, (i + 1) % size) for i in range(size if wrap else size - 1)]
        down = [(j, i) for i, j in up]
        last = lax.slice_in_dim(x, length - width, length, axis=dim)
        leading = lax.slice_in_dim(x, 0, width, axis=dim)
        before = lax.ppermute(last, axis, up)
        after = lax.ppermute(leading, axis, down)
        x = jnp.concatenate([before, x, after], axis=dim)
    return x


def tile_terms(perturb, weight, drive):
    weighted = (perturb.astype(jnp.float32) * weight.astype(jnp.float32)[:, None, :]).astype(
        jnp.bfloat16
    )
    gram_matrix = jnp.einsum("tko,tlo->tkl", weighted, perturb, preferred_element_type=jnp.float32)
    drive_vector = jnp.einsum("tko,to->tk", perturb, drive, preferred_element_type=jnp.float32)
    return (gram_matrix, drive_vector)


def transform_weights(curvature, drive_total, members):
    frob_scale = jnp.sqrt(jnp.sum(curvature * curvature, axis=(1, 2)))
    identity = jnp.eye(members, dtype=jnp.float32)[None]
    current = curvature / frob_scale[:, None, None]
    inverse = jnp.broadcast_to(identity, curvature.shape)
    for _ in range(NS_ITERS):
        middle = 1.5 * identity - 0.5 * jnp.einsum(
            "tij,tjk->tik", inverse, current, precision=lax.Precision.HIGHEST
        )
        current = jnp.einsum("tij,tjk->tik", current, middle, precision=lax.Precision.HIGHEST)
        inverse = jnp.einsum("tij,tjk->tik", middle, inverse, precision=lax.Precision.HIGHEST)
    spread_part = jnp.sqrt((members - 1.0) / frob_scale)[:, None, None] * inverse
    half_step = jnp.einsum("tij,tj->ti", inverse, drive_total, precision=lax.Precision.HIGHEST)
    ensemble_mean_portion = (
        jnp.einsum("tij,tj->ti", inverse, half_step, precision=lax.Precision.HIGHEST)
        / frob_scale[:, None]
    )
    return spread_part + ensemble_mean_portion[:, :, None]


def general_device(
    prior_member_stack,
    zonal_stability_ratio,
    meridional_stability_ratio,
    obs_perturb,
    innovation,
    inverse_error_variance,
    obs_count,
    neighbours,
    localization,
):
    members_dev, channels, row_count, lon_count = prior_member_stack.shape
    mem_count = lax.axis_size("mem")
    lat_count = lax.axis_size("lat")
    lon_strip = lon_count // (mem_count * lat_count)
    members = members_dev * mem_count
    lat_total = row_count * lat_count
    east_neighbour = jnp.roll(prior_member_stack, -1, axis=-1)
    eastward_flux = (
        jnp.maximum(zonal_stability_ratio, 0.0) * prior_member_stack
        + jnp.minimum(zonal_stability_ratio, 0.0) * east_neighbour
    )
    divergence_x = eastward_flux - jnp.roll(eastward_flux, 1, axis=-1)
    stacked = jnp.concatenate(
        [
            prior_member_stack.reshape(members_dev * channels, row_count, lon_count),
            meridional_stability_ratio[None],
        ],
        axis=0,
    )
    padded = extended(stacked, (("lat", 1),), 1, False)
    fields_ext = padded[:-1].reshape(members_dev, channels, row_count + 2, lon_count)
    north_ext = padded[-1, :-1]
    flux_north = (
        jnp.maximum(north_ext, 0.0) * fields_ext[:, :, : row_count + 1]
        + jnp.minimum(north_ext, 0.0) * fields_ext[:, :, 1:]
    )
    transported_quantities = (
        prior_member_stack - divergence_x - (flux_north[:, :, 1:] - flux_north[:, :, :-1])
    )
    rows_last = jnp.swapaxes(transported_quantities, 2, 3)
    moved = rows_last.reshape(1, members_dev, channels, lon_count, row_count)
    arrived = lax.all_to_all(moved, ("mem", "lat"), split_axis=3, concat_axis=0, tiled=True)
    arrived = arrived.reshape(mem_count, lat_count, members_dev, channels, lon_strip, row_count)
    arrived = jnp.transpose(arrived, (0, 2, 3, 4, 1, 5)).reshape(
        members, channels, lon_strip, lat_total
    )
    blocks_per_processor, obs_cap = innovation.shape
    neigh_count = neighbours.shape[1]
    window_tiles = 3 * blocks_per_processor
    is_valid = (
        lax.broadcasted_iota(jnp.int32, (blocks_per_processor, obs_cap), 1) < obs_count[:, None]
    )
    obs_weight = jnp.where(is_valid, inverse_error_variance, 0.0).astype(jnp.bfloat16)
    obs_drive = jnp.where(is_valid, inverse_error_variance * innovation, 0.0).astype(jnp.bfloat16)
    window_slots = lax.broadcasted_iota(jnp.int32, (blocks_per_processor, window_tiles), 1)
    combine = jnp.zeros((blocks_per_processor, window_tiles), jnp.float32)
    for slot_index in range(neigh_count):
        combine = combine + jnp.where(
            neighbours[:, slot_index, None] == window_slots, localization[:, slot_index, None], 0.0
        )
    observed = jnp.concatenate([obs_perturb, obs_weight[:, None, :], obs_drive[:, None, :]], axis=1)
    received = extended(observed, ((("mem", "lat"), 0),), blocks_per_processor, True)
    gram_matrix, drive_vector = tile_terms(
        received[:, :members], received[:, members], received[:, members + 1]
    )
    window = jnp.concatenate([gram_matrix, drive_vector[:, None, :]], axis=1)
    gathered = jnp.einsum("ts,skl->tkl", combine, window, precision=lax.Precision.HIGHEST)
    curvature = (members - 1.0) * jnp.eye(members, dtype=jnp.float32)[None] + gathered[:, :members]
    drive_total = gathered[:, members]
    weights = transform_weights(curvature, drive_total, members)
    grid = arrived.reshape(
        members, channels, lon_strip, blocks_per_processor, lat_total // blocks_per_processor
    )
    member_mean = jnp.mean(grid, axis=0)
    anomaly = grid - member_mean
    update = jnp.einsum("icxtr,tij->jcxtr", anomaly, weights, precision=lax.Precision.HIGHEST)
    return (member_mean + update).reshape(members, channels, lon_strip, lat_total)


def swap_lane_groups(blocks, lane):
    blocks = list(blocks)
    count = len(blocks)
    width = lane.shape[1] // count
    bit = 1
    while bit < count:
        keep = (lane // width) & bit == 0
        for k in range(count):
            if k & bit == 0:
                a, b = blocks[k], blocks[k | bit]
                blocks[k] = jnp.where(keep, a, pltpu.roll(b, bit * width, 1))
                blocks[k | bit] = jnp.where(keep, pltpu.roll(a, lane.shape[1] - bit * width, 1), b)
        bit *= 2
    return blocks


def advance_kernel(prior_ref, zonal_ref, north_ref, south_c_ref, below_ref, above_ref, out_ref):
    pair, channels, rows, lons = prior_ref.shape
    zonal, north = zonal_ref[...], north_ref[...]
    z_pos, z_neg = jnp.maximum(zonal, 0.0), jnp.minimum(zonal, 0.0)
    n_pos, n_neg = jnp.maximum(north, 0.0), jnp.minimum(north, 0.0)
    south = south_c_ref[...]
    s_pos, s_neg = jnp.maximum(south, 0.0), jnp.minimum(south, 0.0)
    row = lax.broadcasted_iota(jnp.int32, (rows, lons), 0)
    lane = lax.broadcasted_iota(jnp.int32, (pair * rows, 128), 1)

    def advanced(i, c):
        p = prior_ref[i, c]
        east = pltpu.roll(p, lons - 1, 1)
        fe = z_pos * p + z_neg * east
        above = jnp.where(row == rows - 1, above_ref[i, c : c + 1, :], pltpu.roll(p, rows - 1, 0))
        fn = n_pos * p + n_neg * above
        face = s_pos * below_ref[i, c : c + 1, :] + s_neg * p[0:1]
        fs = jnp.where(row == 0, face, pltpu.roll(fn, 1, 0))
        return p - (fe - pltpu.roll(fe, 1, 1)) - (fn - fs)

    for h in range(channels // 8):
        whole = [
            jnp.concatenate([advanced(i, 8 * h + k) for i in range(pair)], axis=0)
            for k in range(8)
        ]
        for q in range(lons // 128):
            moved = swap_lane_groups([w[:, q * 128 : (q + 1) * 128] for w in whole], lane)
            for s in range(8):
                out_ref[q * 8 + s, :, h * 128 : (h + 1) * 128] = moved[s].astype(jnp.bfloat16)


def gram_kernel(perturb_ref, innovation_ref, variance_ref, count_ref, out_ref):
    t = pl.program_id(0)
    perturb = perturb_ref[0]
    members, slots = perturb.shape
    valid = lax.broadcasted_iota(jnp.int32, (1, slots), 1) < count_ref[t]
    variance = variance_ref[pl.ds(t, 1), :]
    weight = jnp.where(valid, variance, 0.0).astype(jnp.bfloat16)
    drive = jnp.where(valid, variance * innovation_ref[pl.ds(t, 1), :], 0.0).astype(jnp.bfloat16)
    weighted = (perturb.astype(jnp.float32) * weight.astype(jnp.float32)).astype(jnp.bfloat16)
    first = lax.broadcasted_iota(jnp.int32, (16, slots), 0) == 0
    extra = jnp.where(first, drive.astype(jnp.float32), 0.0).astype(jnp.bfloat16)
    left = jnp.concatenate([weighted, extra], axis=0)
    both = lax.dot_general(
        left, perturb, (((1,), (1,)), ((), ())), preferred_element_type=jnp.float32
    )
    out_ref[0] = both[: members + 8]


def split(x):
    hi = x.astype(jnp.bfloat16)
    return hi, (x - hi.astype(jnp.float32)).astype(jnp.bfloat16)


def dot(a, b):
    return jnp.dot(a, b, preferred_element_type=jnp.float32)


def analysis_kernel(bands, rows, tile_rows, weights_ref, arrived_ref, out_ref, held):
    step = pl.program_id(0)
    members = weights_ref.shape[1]
    wide = members * rows
    per_band = rows // tile_rows

    @pl.when(step < bands)
    def _():
        pick_row = lax.broadcasted_iota(jnp.int32, (wide, per_band * members), 0)
        pick_col = lax.broadcasted_iota(jnp.int32, (wide, per_band * members), 1)
        source = (pick_row % rows) // tile_rows * members + pick_row // rows
        pick = jnp.where(pick_col == source, 1.0, 0.0).astype(jnp.bfloat16)
        spread_row = lax.broadcasted_iota(jnp.int32, (members, wide), 0)
        spread_col = lax.broadcasted_iota(jnp.int32, (members, wide), 1)
        spread = jnp.where(spread_col // rows == spread_row, 1.0, 0.0).astype(jnp.bfloat16)
        here = lax.broadcasted_iota(jnp.int32, (wide, wide), 0) % rows
        there = lax.broadcasted_iota(jnp.int32, (wide, wide), 1) % rows
        diagonal = here == there
        mine = weights_ref[...].reshape(per_band * members, members)
        fields = arrived_ref[...].reshape(wide, arrived_ref.shape[-1])
        total = None
        for part in split(mine):
            tall = dot(pick, part).astype(jnp.bfloat16)
            full = jnp.where(diagonal, dot(tall, spread), 0.0).astype(jnp.bfloat16)
            term = dot(full, fields)
            total = term if total is None else total + term
        where = pl.ds(pl.multiple_of(step * rows, rows), rows)
        held[:, where, :] = total.reshape(members, rows, fields.shape[-1])

    @pl.when(step >= bands)
    def _():
        count, channels, strip, lat = out_ref.shape
        for k in range(count):
            j = (step - bands) * count + k
            out_ref[k] = held[j].T.reshape(channels, strip, lat)


def exchange_kernel(sent_ref, got_ref, local_sem, send_sems, recv_sems):
    lat_count = lax.axis_size("lat")
    count = lax.axis_size("mem") * lat_count
    me = lax.axis_index("mem") * lat_count + lax.axis_index("lat")

    def place(d):
        return {"mem": d // lat_count, "lat": d % lat_count}

    barrier = pltpu.get_barrier_semaphore()

    def greet(k, carry):
        pl.semaphore_signal(
            barrier, inc=1, device_id=place((me + k) % count), device_id_type=pl.DeviceIdType.MESH
        )
        return carry

    lax.fori_loop(1, count, greet, 0)
    pl.semaphore_wait(barrier, count - 1)
    own = pltpu.make_async_copy(sent_ref.at[me], got_ref.at[me], local_sem)
    own.start()

    def sending(k):
        to = (me + k) % count
        return pltpu.make_async_remote_copy(
            src_ref=sent_ref.at[to],
            dst_ref=got_ref.at[me],
            send_sem=send_sems.at[k],
            recv_sem=recv_sems.at[k],
            device_id=place(to),
            device_id_type=pl.DeviceIdType.MESH,
        )

    def arriving(k):
        origin = (me - k + count) % count
        return pltpu.make_async_remote_copy(
            src_ref=sent_ref.at[origin],
            dst_ref=got_ref.at[origin],
            send_sem=send_sems.at[k],
            recv_sem=recv_sems.at[k],
            device_id=place(origin),
            device_id_type=pl.DeviceIdType.MESH,
        )

    def begin(k, carry):
        sending(k).start()
        return carry

    def finish(k, carry):
        sending(k).wait_send()
        arriving(k).wait_recv()
        return carry

    lax.fori_loop(1, count, begin, 0)
    lax.fori_loop(1, count, finish, 0)
    own.wait()


def shifted(x, axis, wrap):
    size = lax.axis_size(axis)
    up = [(i, (i + 1) % size) for i in range(size if wrap else size - 1)]
    down = [(j, i) for i, j in up]
    return up, down


def fast_device(
    prior_member_stack,
    zonal_stability_ratio,
    meridional_stability_ratio,
    obs_perturb,
    innovation,
    inverse_error_variance,
    obs_count,
    neighbours,
    localization,
):
    members_dev, channels, row_count, lon_count = prior_member_stack.shape
    mem_count = lax.axis_size("mem")
    lat_count = lax.axis_size("lat")
    devices = mem_count * lat_count
    strip = lon_count // devices
    members = members_dev * mem_count
    lat_total = row_count * lat_count
    tiles, slots = innovation.shape
    neigh_count = neighbours.shape[1]
    tile_rows = lat_total // tiles
    params = pltpu.CompilerParams(vmem_limit_bytes=VMEM_BYTES)

    up, down = shifted(prior_member_stack, "lat", False)
    below = lax.ppermute(prior_member_stack[:, :, row_count - 1, :], "lat", up)
    above = lax.ppermute(prior_member_stack[:, :, 0, :], "lat", down)
    south_c = lax.ppermute(meridional_stability_ratio[row_count - 1 :], "lat", up)

    gram = pl.pallas_call(
        gram_kernel,
        grid=(tiles,),
        out_shape=jax.ShapeDtypeStruct((tiles, members + 8, members), jnp.float32),
        in_specs=[
            pl.BlockSpec((1, members, slots), lambda t: (t, 0, 0)),
            pl.BlockSpec((tiles, slots), lambda t: (0, 0)),
            pl.BlockSpec((tiles, slots), lambda t: (0, 0)),
            pl.BlockSpec(memory_space=pltpu.SMEM),
        ],
        out_specs=pl.BlockSpec((1, members + 8, members), lambda t: (t, 0, 0)),
        compiler_params=params,
        name="gram",
    )(obs_perturb, innovation, inverse_error_variance, obs_count)
    ring = ("mem", "lat")
    up, down = shifted(gram, ring, True)
    window = jnp.concatenate(
        [lax.ppermute(gram, ring, up), gram, lax.ppermute(gram, ring, down)], axis=0
    )

    pair = 2
    sent = pl.pallas_call(
        advance_kernel,
        grid=(members_dev // pair,),
        out_shape=jax.ShapeDtypeStruct(
            (devices, members_dev * row_count, channels * strip), jnp.bfloat16
        ),
        in_specs=[
            pl.BlockSpec((pair, channels, row_count, lon_count), lambda g: (g, 0, 0, 0)),
            pl.BlockSpec((row_count, lon_count), lambda g: (0, 0)),
            pl.BlockSpec((row_count, lon_count), lambda g: (0, 0)),
            pl.BlockSpec((1, lon_count), lambda g: (0, 0)),
            pl.BlockSpec((pair, channels, lon_count), lambda g: (g, 0, 0)),
            pl.BlockSpec((pair, channels, lon_count), lambda g: (g, 0, 0)),
        ],
        out_specs=pl.BlockSpec((devices, pair * row_count, channels * strip), lambda g: (0, g, 0)),
        compiler_params=params,
        name="advance",
    )(
        prior_member_stack,
        zonal_stability_ratio,
        meridional_stability_ratio,
        south_c,
        below,
        above,
    )

    arrived = pl.pallas_call(
        exchange_kernel,
        out_shape=jax.ShapeDtypeStruct(sent.shape, sent.dtype),
        in_specs=[pl.BlockSpec(memory_space=pl.ANY)],
        out_specs=pl.BlockSpec(memory_space=pl.ANY),
        scratch_shapes=[
            pltpu.SemaphoreType.DMA(()),
            pltpu.SemaphoreType.DMA((devices,)),
            pltpu.SemaphoreType.DMA((devices,)),
        ],
        compiler_params=pltpu.CompilerParams(collective_id=0, has_side_effects=True),
        name="exchange",
    )(sent)

    window_slots = lax.broadcasted_iota(jnp.int32, (tiles, 3 * tiles), 1)
    combine = jnp.zeros((tiles, 3 * tiles), jnp.float32)
    for n in range(neigh_count):
        combine = combine + jnp.where(
            neighbours[:, n, None] == window_slots, localization[:, n, None], 0.0
        )
    gathered = jnp.einsum("ts,skl->tkl", combine, window, precision=lax.Precision.HIGHEST)
    curvature = (members - 1.0) * jnp.eye(members, dtype=jnp.float32)[None] + gathered[:, :members]
    weights = transform_weights(curvature, gathered[:, members], members)
    folded = jnp.swapaxes(
        1.0 / members + weights - jnp.mean(weights, axis=1, keepdims=True), 1, 2
    )

    per_band = row_count // tile_rows
    j_block = 8
    j_steps = members // j_block
    last = lat_count - 1
    return pl.pallas_call(
        lambda *refs: analysis_kernel(lat_count, row_count, tile_rows, *refs),
        grid=(lat_count + j_steps,),
        out_shape=jax.ShapeDtypeStruct((members, channels, strip, lat_total), jnp.float32),
        in_specs=[
            pl.BlockSpec((per_band, members, members), lambda s: (jnp.minimum(s, last), 0, 0)),
            pl.BlockSpec(
                (mem_count, 1, members_dev * row_count, channels * strip),
                lambda s: (0, jnp.minimum(s, last), 0, 0),
            ),
        ],
        out_specs=pl.BlockSpec(
            (j_block, channels, strip, lat_total),
            lambda s: (jnp.maximum(s - lat_count, 0), 0, 0, 0),
        ),
        scratch_shapes=[pltpu.VMEM((members, lat_total, channels * strip), jnp.float32)],
        compiler_params=params,
        name="analysis",
    )(folded, arrived.reshape(mem_count, lat_count, members_dev * row_count, channels * strip))


def per_device(prior_member_stack, *rest):
    members_dev, channels, row_count, lon_count = prior_member_stack.shape
    lat_count = lax.axis_size("lat")
    devices = lax.axis_size("mem") * lat_count
    tiles = rest[3].shape[0]
    tile_rows = row_count * lat_count // tiles
    fits = (
        lon_count == 16 * devices
        and channels % 8 == 0
        and row_count == 8
        and tile_rows in (1, 2, 4, 8)
        and members_dev % 2 == 0
    )
    return (fast_device if fits else general_device)(prior_member_stack, *rest)


def solution(mesh):
    in_specs = (
        P("mem", None, "lat", None),
        P("lat", None),
        P("lat", None),
        P(("mem", "lat"), None, None),
        P(("mem", "lat"), None),
        P(("mem", "lat"), None),
        P(("mem", "lat")),
        P(("mem", "lat"), None),
        P(("mem", "lat"), None),
    )
    out_specs = P(None, None, ("mem", "lat"), None)
    return jax.shard_map(
        per_device, mesh=mesh, in_specs=in_specs, out_specs=out_specs, check_vma=False
    )
```

```python
import jax
import jax.numpy as jnp
from jax import lax
from jax.experimental import pallas as pl
from jax.experimental.pallas import tpu as pltpu
from jax.sharding import PartitionSpec as P

NS_ITERS = 5
VMEM_BYTES = 48 * 1024 * 1024


def extended(x, sides, width, wrap):
    for axis, dim in sides:
        size, length = (lax.axis_size(axis), x.shape[dim])
        up = [(i, (i + 1) % size) for i in range(size if wrap else size - 1)]
        down = [(j, i) for i, j in up]
        last = lax.slice_in_dim(x, length - width, length, axis=dim)
        leading = lax.slice_in_dim(x, 0, width, axis=dim)
        before = lax.ppermute(last, axis, up)
        after = lax.ppermute(leading, axis, down)
        x = jnp.concatenate([before, x, after], axis=dim)
    return x


def tile_terms(perturb, weight, drive):
    weighted = (perturb.astype(jnp.float32) * weight.astype(jnp.float32)[:, None, :]).astype(
        jnp.bfloat16
    )
    gram_matrix = jnp.einsum("tko,tlo->tkl", weighted, perturb, preferred_element_type=jnp.float32)
    drive_vector = jnp.einsum("tko,to->tk", perturb, drive, preferred_element_type=jnp.float32)
    return (gram_matrix, drive_vector)


def transform_weights(curvature, drive_total, members):
    frob_scale = jnp.sqrt(jnp.sum(curvature * curvature, axis=(1, 2)))
    identity = jnp.eye(members, dtype=jnp.float32)[None]
    current = curvature / frob_scale[:, None, None]
    inverse = jnp.broadcast_to(identity, curvature.shape)
    for _ in range(NS_ITERS):
        middle = 1.5 * identity - 0.5 * jnp.einsum(
            "tij,tjk->tik", inverse, current, precision=lax.Precision.HIGHEST
        )
        current = jnp.einsum("tij,tjk->tik", current, middle, precision=lax.Precision.HIGHEST)
        inverse = jnp.einsum("tij,tjk->tik", middle, inverse, precision=lax.Precision.HIGHEST)
    spread_part = jnp.sqrt((members - 1.0) / frob_scale)[:, None, None] * inverse
    half_step = jnp.einsum("tij,tj->ti", inverse, drive_total, precision=lax.Precision.HIGHEST)
    ensemble_mean_portion = (
        jnp.einsum("tij,tj->ti", inverse, half_step, precision=lax.Precision.HIGHEST)
        / frob_scale[:, None]
    )
    return spread_part + ensemble_mean_portion[:, :, None]


def general_device(
    prior_member_stack,
    zonal_stability_ratio,
    meridional_stability_ratio,
    obs_perturb,
    innovation,
    inverse_error_variance,
    obs_count,
    neighbours,
    localization,
):
    members_dev, channels, row_count, lon_count = prior_member_stack.shape
    mem_count = lax.axis_size("mem")
    lat_count = lax.axis_size("lat")
    lon_strip = lon_count // (mem_count * lat_count)
    members = members_dev * mem_count
    lat_total = row_count * lat_count
    east_neighbour = jnp.roll(prior_member_stack, -1, axis=-1)
    eastward_flux = (
        jnp.maximum(zonal_stability_ratio, 0.0) * prior_member_stack
        + jnp.minimum(zonal_stability_ratio, 0.0) * east_neighbour
    )
    divergence_x = eastward_flux - jnp.roll(eastward_flux, 1, axis=-1)
    stacked = jnp.concatenate(
        [
            prior_member_stack.reshape(members_dev * channels, row_count, lon_count),
            meridional_stability_ratio[None],
        ],
        axis=0,
    )
    padded = extended(stacked, (("lat", 1),), 1, False)
    fields_ext = padded[:-1].reshape(members_dev, channels, row_count + 2, lon_count)
    north_ext = padded[-1, :-1]
    flux_north = (
        jnp.maximum(north_ext, 0.0) * fields_ext[:, :, : row_count + 1]
        + jnp.minimum(north_ext, 0.0) * fields_ext[:, :, 1:]
    )
    transported_quantities = (
        prior_member_stack - divergence_x - (flux_north[:, :, 1:] - flux_north[:, :, :-1])
    )
    rows_last = jnp.swapaxes(transported_quantities, 2, 3)
    moved = rows_last.reshape(1, members_dev, channels, lon_count, row_count)
    arrived = lax.all_to_all(moved, ("mem", "lat"), split_axis=3, concat_axis=0, tiled=True)
    arrived = arrived.reshape(mem_count, lat_count, members_dev, channels, lon_strip, row_count)
    arrived = jnp.transpose(arrived, (0, 2, 3, 4, 1, 5)).reshape(
        members, channels, lon_strip, lat_total
    )
    blocks_per_processor, obs_cap = innovation.shape
    neigh_count = neighbours.shape[1]
    window_tiles = 3 * blocks_per_processor
    is_valid = (
        lax.broadcasted_iota(jnp.int32, (blocks_per_processor, obs_cap), 1) < obs_count[:, None]
    )
    obs_weight = jnp.where(is_valid, inverse_error_variance, 0.0).astype(jnp.bfloat16)
    obs_drive = jnp.where(is_valid, inverse_error_variance * innovation, 0.0).astype(jnp.bfloat16)
    window_slots = lax.broadcasted_iota(jnp.int32, (blocks_per_processor, window_tiles), 1)
    combine = jnp.zeros((blocks_per_processor, window_tiles), jnp.float32)
    for slot_index in range(neigh_count):
        combine = combine + jnp.where(
            neighbours[:, slot_index, None] == window_slots, localization[:, slot_index, None], 0.0
        )
    observed = jnp.concatenate([obs_perturb, obs_weight[:, None, :], obs_drive[:, None, :]], axis=1)
    received = extended(observed, ((("mem", "lat"), 0),), blocks_per_processor, True)
    gram_matrix, drive_vector = tile_terms(
        received[:, :members], received[:, members], received[:, members + 1]
    )
    window = jnp.concatenate([gram_matrix, drive_vector[:, None, :]], axis=1)
    gathered = jnp.einsum("ts,skl->tkl", combine, window, precision=lax.Precision.HIGHEST)
    curvature = (members - 1.0) * jnp.eye(members, dtype=jnp.float32)[None] + gathered[:, :members]
    drive_total = gathered[:, members]
    weights = transform_weights(curvature, drive_total, members)
    grid = arrived.reshape(
        members, channels, lon_strip, blocks_per_processor, lat_total // blocks_per_processor
    )
    member_mean = jnp.mean(grid, axis=0)
    anomaly = grid - member_mean
    update = jnp.einsum("icxtr,tij->jcxtr", anomaly, weights, precision=lax.Precision.HIGHEST)
    return (member_mean + update).reshape(members, channels, lon_strip, lat_total)


def swap_lane_groups(blocks, lane):
    blocks = list(blocks)
    count = len(blocks)
    width = lane.shape[1] // count
    bit = 1
    while bit < count:
        keep = (lane // width) & bit == 0
        for k in range(count):
            if k & bit == 0:
                a, b = blocks[k], blocks[k | bit]
                blocks[k] = jnp.where(keep, a, pltpu.roll(b, bit * width, 1))
                blocks[k | bit] = jnp.where(keep, pltpu.roll(a, lane.shape[1] - bit * width, 1), b)
        bit *= 2
    return blocks


def advance(prior_ref, zonal_ref, north_ref, south_c_ref, below_ref, above_ref, out_ref, step):
    pair, channels, rows, lons = prior_ref.shape
    zonal, north = zonal_ref[...], north_ref[...]
    z_pos, z_neg = jnp.maximum(zonal, 0.0), jnp.minimum(zonal, 0.0)
    n_pos, n_neg = jnp.maximum(north, 0.0), jnp.minimum(north, 0.0)
    south = south_c_ref[...]
    s_pos, s_neg = jnp.maximum(south, 0.0), jnp.minimum(south, 0.0)
    row = lax.broadcasted_iota(jnp.int32, (rows, lons), 0)
    lane = lax.broadcasted_iota(jnp.int32, (pair * rows, 128), 1)
    where = pl.ds(pl.multiple_of(step * pair * rows, pair * rows), pair * rows)

    def advanced(i, c):
        p = prior_ref[i, c]
        east = pltpu.roll(p, lons - 1, 1)
        fe = z_pos * p + z_neg * east
        above = jnp.where(row == rows - 1, above_ref[i, c : c + 1, :], pltpu.roll(p, rows - 1, 0))
        fn = n_pos * p + n_neg * above
        face = s_pos * below_ref[i, c : c + 1, :] + s_neg * p[0:1]
        fs = jnp.where(row == 0, face, pltpu.roll(fn, 1, 0))
        return p - (fe - pltpu.roll(fe, 1, 1)) - (fn - fs)

    for h in range(channels // 8):
        whole = [
            jnp.concatenate([advanced(i, 8 * h + k) for i in range(pair)], axis=0)
            for k in range(8)
        ]
        for q in range(lons // 128):
            moved = swap_lane_groups([w[:, q * 128 : (q + 1) * 128] for w in whole], lane)
            for s in range(8):
                out_ref[q * 8 + s, where, h * 128 : (h + 1) * 128] = moved[s].astype(jnp.bfloat16)


def gram_kernel(perturb_ref, innovation_ref, variance_ref, count_ref, out_ref):
    t = pl.program_id(0)
    perturb = perturb_ref[0]
    members, slots = perturb.shape
    valid = lax.broadcasted_iota(jnp.int32, (1, slots), 1) < count_ref[t]
    variance = variance_ref[pl.ds(t, 1), :]
    weight = jnp.where(valid, variance, 0.0).astype(jnp.bfloat16)
    drive = jnp.where(valid, variance * innovation_ref[pl.ds(t, 1), :], 0.0).astype(jnp.bfloat16)
    weighted = (perturb.astype(jnp.float32) * weight.astype(jnp.float32)).astype(jnp.bfloat16)
    first = lax.broadcasted_iota(jnp.int32, (16, slots), 0) == 0
    extra = jnp.where(first, drive.astype(jnp.float32), 0.0).astype(jnp.bfloat16)
    left = jnp.concatenate([weighted, extra], axis=0)
    both = lax.dot_general(
        left, perturb, (((1,), (1,)), ((), ())), preferred_element_type=jnp.float32
    )
    out_ref[0] = both[: members + 8]


def split(x):
    hi = x.astype(jnp.bfloat16)
    return hi, (x - hi.astype(jnp.float32)).astype(jnp.bfloat16)


def dot(a, b):
    return jnp.dot(a, b, preferred_element_type=jnp.float32)


def analysis_kernel(bands, rows, tile_rows, weights_ref, arrived_ref, out_ref, held):
    step = pl.program_id(0)
    members = weights_ref.shape[1]
    wide = members * rows
    per_band = rows // tile_rows

    @pl.when(step < bands)
    def _():
        pick_row = lax.broadcasted_iota(jnp.int32, (wide, per_band * members), 0)
        pick_col = lax.broadcasted_iota(jnp.int32, (wide, per_band * members), 1)
        source = (pick_row % rows) // tile_rows * members + pick_row // rows
        pick = jnp.where(pick_col == source, 1.0, 0.0).astype(jnp.bfloat16)
        spread_row = lax.broadcasted_iota(jnp.int32, (members, wide), 0)
        spread_col = lax.broadcasted_iota(jnp.int32, (members, wide), 1)
        spread = jnp.where(spread_col // rows == spread_row, 1.0, 0.0).astype(jnp.bfloat16)
        here = lax.broadcasted_iota(jnp.int32, (wide, wide), 0) % rows
        there = lax.broadcasted_iota(jnp.int32, (wide, wide), 1) % rows
        diagonal = here == there
        mine = weights_ref[...].reshape(per_band * members, members)
        fields = arrived_ref[...].reshape(wide, arrived_ref.shape[-1])
        total = None
        for part in split(mine):
            tall = dot(pick, part).astype(jnp.bfloat16)
            full = jnp.where(diagonal, dot(tall, spread), 0.0).astype(jnp.bfloat16)
            term = dot(full, fields)
            total = term if total is None else total + term
        where = pl.ds(pl.multiple_of(step * rows, rows), rows)
        held[:, where, :] = total.reshape(members, rows, fields.shape[-1])

    @pl.when(step >= bands)
    def _():
        count, channels, strip, lat = out_ref.shape
        for k in range(count):
            j = (step - bands) * count + k
            out_ref[k] = held[j].T.reshape(channels, strip, lat)


def iterate(window, neighbours_ref, localization_ref, current, inverse, weights_ref):
    tiles, members = weights_ref.shape[:2]
    row = lax.broadcasted_iota(jnp.int32, (members, members), 0)
    col = lax.broadcasted_iota(jnp.int32, (members, members), 1)
    identity = jnp.where(row == col, 1.0, 0.0)

    def exact(a, b, dims=((1,), (0,))):
        return lax.dot_general(
            a, b, (dims, ((), ())),
            precision=lax.Precision.HIGHEST, preferred_element_type=jnp.float32,
        )

    scales, drives = [], []
    for t in range(tiles):
        total = None
        for n in range(neighbours_ref.shape[1]):
            term = localization_ref[t, n] * window[neighbours_ref[t, n]]
            total = term if total is None else total + term
        curvature = (members - 1.0) * identity + total[:members]
        scale = jnp.sqrt(jnp.sum(curvature * curvature, keepdims=True))
        scales.append(scale)
        drives.append(total[members:])
        current[t] = curvature / scale
        inverse[t] = identity

    def one(_, carry):
        for t in range(tiles):
            now, inv = current[t], inverse[t]
            middle = 1.5 * identity - 0.5 * exact(inv, now)
            current[t] = exact(now, middle)
            inverse[t] = exact(middle, inv)
        return carry

    lax.fori_loop(0, NS_ITERS, one, 0)
    for t in range(tiles):
        inv = inverse[t]
        half = exact(drives[t], inv, ((1,), (1,)))
        shift = exact(half, inv, ((1,), (1,))) / scales[t]
        turned = jnp.sqrt((members - 1.0) / scales[t]) * inv.T + shift[0:1]
        weights_ref[t] = 1.0 / members + turned - jnp.mean(turned, axis=1, keepdims=True)


def transport_kernel(
    prior_ref, zonal_ref, north_ref, south_c_ref, below_ref, above_ref, gram_ref,
    neighbours_ref, localization_ref, got_ref, weights_ref,
    sent, window, current, inverse,
    own_sem, gram_own_sem, send_sems, recv_sems, gram_send_sems, gram_recv_sems,
):
    step, steps = pl.program_id(0), pl.num_programs(0)
    lat_count = lax.axis_size("lat")
    count = lax.axis_size("mem") * lat_count
    me = lax.axis_index("mem") * lat_count + lax.axis_index("lat")
    tiles = gram_ref.shape[0]
    chunks = send_sems.shape[0]
    per_chunk = steps // chunks
    chunk_rows = sent.shape[1] // chunks
    barrier = pltpu.get_barrier_semaphore()

    def place(d):
        return {"mem": d // lat_count, "lat": d % lat_count}

    def sending(chunk, k):
        to = (me + k) % count
        rows = pl.ds(pl.multiple_of(chunk * chunk_rows, chunk_rows), chunk_rows)
        return pltpu.make_async_remote_copy(
            src_ref=sent.at[to, rows],
            dst_ref=got_ref.at[me, rows],
            send_sem=send_sems.at[chunk, k],
            recv_sem=recv_sems.at[chunk, k],
            device_id=place(to),
            device_id_type=pl.DeviceIdType.MESH,
        )

    def arriving(chunk, k):
        origin = (me - k + count) % count
        rows = pl.ds(pl.multiple_of(chunk * chunk_rows, chunk_rows), chunk_rows)
        return pltpu.make_async_remote_copy(
            src_ref=sent.at[origin, rows],
            dst_ref=got_ref.at[origin, rows],
            send_sem=send_sems.at[chunk, k],
            recv_sem=recv_sems.at[chunk, k],
            device_id=place(origin),
            device_id_type=pl.DeviceIdType.MESH,
        )

    def gram_copy(side):
        to = (me + 1) % count if side == 0 else (me - 1 + count) % count
        return pltpu.make_async_remote_copy(
            src_ref=gram_ref,
            dst_ref=window.at[pl.ds(2 * tiles * side, tiles)],
            send_sem=gram_send_sems.at[side],
            recv_sem=gram_recv_sems.at[side],
            device_id=place(to),
            device_id_type=pl.DeviceIdType.MESH,
        )

    gram_own = pltpu.make_async_copy(gram_ref, window.at[pl.ds(tiles, tiles)], gram_own_sem)
    own = pltpu.make_async_copy(sent.at[me], got_ref.at[me], own_sem)

    @pl.when(step == 0)
    def _():
        def greet(k, carry):
            pl.semaphore_signal(
                barrier, inc=1, device_id=place((me + k) % count),
                device_id_type=pl.DeviceIdType.MESH,
            )
            return carry

        lax.fori_loop(1, count, greet, 0)
        pl.semaphore_wait(barrier, count - 1)
        gram_copy(0).start()
        gram_copy(1).start()
        gram_own.start()

    advance(
        prior_ref, zonal_ref, north_ref, south_c_ref, below_ref, above_ref, sent, step
    )

    @pl.when(step % per_chunk == per_chunk - 1)
    def _():
        def begin(k, carry):
            sending(step // per_chunk, k).start()
            return carry

        lax.fori_loop(1, count, begin, 0)

    @pl.when(step == steps - 1)
    def _():
        own.start()
        gram_own.wait()
        gram_copy(0).wait()
        gram_copy(1).wait()
        iterate(window, neighbours_ref, localization_ref, current, inverse, weights_ref)

        def finish(i, carry):
            chunk, k = i // (count - 1), i % (count - 1) + 1
            sending(chunk, k).wait_send()
            arriving(chunk, k).wait_recv()
            return carry

        lax.fori_loop(0, chunks * (count - 1), finish, 0)
        own.wait()


def shifted(axis, wrap):
    size = lax.axis_size(axis)
    up = [(i, (i + 1) % size) for i in range(size if wrap else size - 1)]
    down = [(j, i) for i, j in up]
    return up, down


def fast_device(
    prior_member_stack,
    zonal_stability_ratio,
    meridional_stability_ratio,
    obs_perturb,
    innovation,
    inverse_error_variance,
    obs_count,
    neighbours,
    localization,
):
    members_dev, channels, row_count, lon_count = prior_member_stack.shape
    mem_count = lax.axis_size("mem")
    lat_count = lax.axis_size("lat")
    devices = mem_count * lat_count
    strip = lon_count // devices
    members = members_dev * mem_count
    lat_total = row_count * lat_count
    tiles, slots = innovation.shape
    tile_rows = lat_total // tiles
    params = pltpu.CompilerParams(vmem_limit_bytes=VMEM_BYTES)

    up, down = shifted("lat", False)
    edges = (
        prior_member_stack[:, :, row_count - 1, :],
        prior_member_stack[:, :, 0, :],
        meridional_stability_ratio[row_count - 1 :],
    )
    *edges, obs_count = lax.optimization_barrier((*edges, obs_count))
    below = lax.ppermute(edges[0], "lat", up)
    above = lax.ppermute(edges[1], "lat", down)
    south_c = lax.ppermute(edges[2], "lat", up)

    gram = pl.pallas_call(
        gram_kernel,
        grid=(tiles,),
        out_shape=jax.ShapeDtypeStruct((tiles, members + 8, members), jnp.float32),
        in_specs=[
            pl.BlockSpec((1, members, slots), lambda t: (t, 0, 0)),
            pl.BlockSpec((tiles, slots), lambda t: (0, 0)),
            pl.BlockSpec((tiles, slots), lambda t: (0, 0)),
            pl.BlockSpec(memory_space=pltpu.SMEM),
        ],
        out_specs=pl.BlockSpec((1, members + 8, members), lambda t: (t, 0, 0)),
        compiler_params=params,
        cost_estimate=pl.CostEstimate(
            flops=4 * obs_perturb.size * members, bytes_accessed=4 * obs_perturb.size, transcendentals=0
        ),
        name="gram",
    )(obs_perturb, innovation, inverse_error_variance, obs_count)

    pair, chunks = 2, 4
    wire = (devices, members_dev * row_count, channels * strip)
    square = (tiles, members, members)
    arrived, folded = pl.pallas_call(
        transport_kernel,
        grid=(members_dev // pair,),
        out_shape=(
            jax.ShapeDtypeStruct(wire, jnp.bfloat16),
            jax.ShapeDtypeStruct(square, jnp.float32),
        ),
        in_specs=[
            pl.BlockSpec((pair, channels, row_count, lon_count), lambda g: (g, 0, 0, 0)),
            pl.BlockSpec((row_count, lon_count), lambda g: (0, 0)),
            pl.BlockSpec((row_count, lon_count), lambda g: (0, 0)),
            pl.BlockSpec((1, lon_count), lambda g: (0, 0)),
            pl.BlockSpec((pair, channels, lon_count), lambda g: (g, 0, 0)),
            pl.BlockSpec((pair, channels, lon_count), lambda g: (g, 0, 0)),
            pl.BlockSpec(memory_space=pltpu.VMEM),
            pl.BlockSpec(memory_space=pltpu.SMEM),
            pl.BlockSpec(memory_space=pltpu.SMEM),
        ],
        out_specs=(
            pl.BlockSpec(memory_space=pl.ANY),
            pl.BlockSpec(square, lambda g: (0, 0, 0)),
        ),
        scratch_shapes=[
            pltpu.VMEM(wire, jnp.bfloat16),
            pltpu.VMEM((3 * tiles, members + 8, members), jnp.float32),
            pltpu.VMEM(square, jnp.float32),
            pltpu.VMEM(square, jnp.float32),
            pltpu.SemaphoreType.DMA(()),
            pltpu.SemaphoreType.DMA(()),
            pltpu.SemaphoreType.DMA((chunks, devices)),
            pltpu.SemaphoreType.DMA((chunks, devices)),
            pltpu.SemaphoreType.DMA((2,)),
            pltpu.SemaphoreType.DMA((2,)),
        ],
        compiler_params=pltpu.CompilerParams(
            collective_id=0, has_side_effects=True, vmem_limit_bytes=VMEM_BYTES
        ),
        name="transport",
    )(
        prior_member_stack,
        zonal_stability_ratio,
        meridional_stability_ratio,
        south_c,
        below,
        above,
        gram,
        neighbours,
        localization,
    )

    per_band = row_count // tile_rows
    j_block = 8
    j_steps = members // j_block
    last = lat_count - 1
    return pl.pallas_call(
        lambda *refs: analysis_kernel(lat_count, row_count, tile_rows, *refs),
        grid=(lat_count + j_steps,),
        out_shape=jax.ShapeDtypeStruct((members, channels, strip, lat_total), jnp.float32),
        in_specs=[
            pl.BlockSpec((per_band, members, members), lambda s: (jnp.minimum(s, last), 0, 0)),
            pl.BlockSpec(
                (mem_count, 1, members_dev * row_count, channels * strip),
                lambda s: (0, jnp.minimum(s, last), 0, 0),
            ),
        ],
        out_specs=pl.BlockSpec(
            (j_block, channels, strip, lat_total),
            lambda s: (jnp.maximum(s - lat_count, 0), 0, 0, 0),
        ),
        scratch_shapes=[pltpu.VMEM((members, lat_total, channels * strip), jnp.float32)],
        compiler_params=params,
        name="analysis",
    )(folded, arrived.reshape(mem_count, lat_count, members_dev * row_count, channels * strip))


def per_device(prior_member_stack, *rest):
    members_dev, channels, row_count, lon_count = prior_member_stack.shape
    lat_count = lax.axis_size("lat")
    devices = lax.axis_size("mem") * lat_count
    tiles = rest[3].shape[0]
    tile_rows = row_count * lat_count // tiles
    fits = (
        lon_count == 16 * devices
        and channels % 8 == 0
        and row_count == 8
        and tile_rows in (1, 2, 4, 8)
        and members_dev % 8 == 0
    )
    return (fast_device if fits else general_device)(prior_member_stack, *rest)


def solution(mesh):
    in_specs = (
        P("mem", None, "lat", None),
        P("lat", None),
        P("lat", None),
        P(("mem", "lat"), None, None),
        P(("mem", "lat"), None),
        P(("mem", "lat"), None),
        P(("mem", "lat")),
        P(("mem", "lat"), None),
        P(("mem", "lat"), None),
    )
    out_specs = P(None, None, ("mem", "lat"), None)
    return jax.shard_map(
        per_device, mesh=mesh, in_specs=in_specs, out_specs=out_specs, check_vma=False
    )
```

```python
import jax
import jax.numpy as jnp
from jax import lax
from jax.experimental import pallas as pl
from jax.experimental.pallas import tpu as pltpu
from jax.sharding import PartitionSpec as P

NS_ITERS = 5
VMEM_BYTES = 48 * 1024 * 1024


def extended(x, sides, width, wrap):
    for axis, dim in sides:
        size, length = (lax.axis_size(axis), x.shape[dim])
        up = [(i, (i + 1) % size) for i in range(size if wrap else size - 1)]
        down = [(j, i) for i, j in up]
        last = lax.slice_in_dim(x, length - width, length, axis=dim)
        leading = lax.slice_in_dim(x, 0, width, axis=dim)
        before = lax.ppermute(last, axis, up)
        after = lax.ppermute(leading, axis, down)
        x = jnp.concatenate([before, x, after], axis=dim)
    return x


def tile_terms(perturb, weight, drive):
    weighted = (perturb.astype(jnp.float32) * weight.astype(jnp.float32)[:, None, :]).astype(
        jnp.bfloat16
    )
    gram_matrix = jnp.einsum("tko,tlo->tkl", weighted, perturb, preferred_element_type=jnp.float32)
    drive_vector = jnp.einsum("tko,to->tk", perturb, drive, preferred_element_type=jnp.float32)
    return (gram_matrix, drive_vector)


def transform_weights(curvature, drive_total, members):
    frob_scale = jnp.sqrt(jnp.sum(curvature * curvature, axis=(1, 2)))
    identity = jnp.eye(members, dtype=jnp.float32)[None]
    current = curvature / frob_scale[:, None, None]
    inverse = jnp.broadcast_to(identity, curvature.shape)
    for _ in range(NS_ITERS):
        middle = 1.5 * identity - 0.5 * jnp.einsum(
            "tij,tjk->tik", inverse, current, precision=lax.Precision.HIGHEST
        )
        current = jnp.einsum("tij,tjk->tik", current, middle, precision=lax.Precision.HIGHEST)
        inverse = jnp.einsum("tij,tjk->tik", middle, inverse, precision=lax.Precision.HIGHEST)
    spread_part = jnp.sqrt((members - 1.0) / frob_scale)[:, None, None] * inverse
    half_step = jnp.einsum("tij,tj->ti", inverse, drive_total, precision=lax.Precision.HIGHEST)
    ensemble_mean_portion = (
        jnp.einsum("tij,tj->ti", inverse, half_step, precision=lax.Precision.HIGHEST)
        / frob_scale[:, None]
    )
    return spread_part + ensemble_mean_portion[:, :, None]


def general_device(
    prior_member_stack,
    zonal_stability_ratio,
    meridional_stability_ratio,
    obs_perturb,
    innovation,
    inverse_error_variance,
    obs_count,
    neighbours,
    localization,
):
    members_dev, channels, row_count, lon_count = prior_member_stack.shape
    mem_count = lax.axis_size("mem")
    lat_count = lax.axis_size("lat")
    lon_strip = lon_count // (mem_count * lat_count)
    members = members_dev * mem_count
    lat_total = row_count * lat_count
    east_neighbour = jnp.roll(prior_member_stack, -1, axis=-1)
    eastward_flux = (
        jnp.maximum(zonal_stability_ratio, 0.0) * prior_member_stack
        + jnp.minimum(zonal_stability_ratio, 0.0) * east_neighbour
    )
    divergence_x = eastward_flux - jnp.roll(eastward_flux, 1, axis=-1)
    stacked = jnp.concatenate(
        [
            prior_member_stack.reshape(members_dev * channels, row_count, lon_count),
            meridional_stability_ratio[None],
        ],
        axis=0,
    )
    padded = extended(stacked, (("lat", 1),), 1, False)
    fields_ext = padded[:-1].reshape(members_dev, channels, row_count + 2, lon_count)
    north_ext = padded[-1, :-1]
    flux_north = (
        jnp.maximum(north_ext, 0.0) * fields_ext[:, :, : row_count + 1]
        + jnp.minimum(north_ext, 0.0) * fields_ext[:, :, 1:]
    )
    transported_quantities = (
        prior_member_stack - divergence_x - (flux_north[:, :, 1:] - flux_north[:, :, :-1])
    )
    rows_last = jnp.swapaxes(transported_quantities, 2, 3)
    moved = rows_last.reshape(1, members_dev, channels, lon_count, row_count)
    arrived = lax.all_to_all(moved, ("mem", "lat"), split_axis=3, concat_axis=0, tiled=True)
    arrived = arrived.reshape(mem_count, lat_count, members_dev, channels, lon_strip, row_count)
    arrived = jnp.transpose(arrived, (0, 2, 3, 4, 1, 5)).reshape(
        members, channels, lon_strip, lat_total
    )
    blocks_per_processor, obs_cap = innovation.shape
    neigh_count = neighbours.shape[1]
    window_tiles = 3 * blocks_per_processor
    is_valid = (
        lax.broadcasted_iota(jnp.int32, (blocks_per_processor, obs_cap), 1) < obs_count[:, None]
    )
    obs_weight = jnp.where(is_valid, inverse_error_variance, 0.0).astype(jnp.bfloat16)
    obs_drive = jnp.where(is_valid, inverse_error_variance * innovation, 0.0).astype(jnp.bfloat16)
    window_slots = lax.broadcasted_iota(jnp.int32, (blocks_per_processor, window_tiles), 1)
    combine = jnp.zeros((blocks_per_processor, window_tiles), jnp.float32)
    for slot_index in range(neigh_count):
        combine = combine + jnp.where(
            neighbours[:, slot_index, None] == window_slots, localization[:, slot_index, None], 0.0
        )
    observed = jnp.concatenate([obs_perturb, obs_weight[:, None, :], obs_drive[:, None, :]], axis=1)
    received = extended(observed, ((("mem", "lat"), 0),), blocks_per_processor, True)
    gram_matrix, drive_vector = tile_terms(
        received[:, :members], received[:, members], received[:, members + 1]
    )
    window = jnp.concatenate([gram_matrix, drive_vector[:, None, :]], axis=1)
    gathered = jnp.einsum("ts,skl->tkl", combine, window, precision=lax.Precision.HIGHEST)
    curvature = (members - 1.0) * jnp.eye(members, dtype=jnp.float32)[None] + gathered[:, :members]
    drive_total = gathered[:, members]
    weights = transform_weights(curvature, drive_total, members)
    grid = arrived.reshape(
        members, channels, lon_strip, blocks_per_processor, lat_total // blocks_per_processor
    )
    member_mean = jnp.mean(grid, axis=0)
    anomaly = grid - member_mean
    update = jnp.einsum("icxtr,tij->jcxtr", anomaly, weights, precision=lax.Precision.HIGHEST)
    return (member_mean + update).reshape(members, channels, lon_strip, lat_total)


def swap_lane_groups(blocks, lane):
    blocks = list(blocks)
    count = len(blocks)
    width = lane.shape[1] // count
    bit = 1
    while bit < count:
        keep = (lane // width) & bit == 0
        for k in range(count):
            if k & bit == 0:
                a, b = blocks[k], blocks[k | bit]
                blocks[k] = jnp.where(keep, a, pltpu.roll(b, bit * width, 1))
                blocks[k | bit] = jnp.where(keep, pltpu.roll(a, lane.shape[1] - bit * width, 1), b)
        bit *= 2
    return blocks


def advance(prior_ref, zonal_ref, north_ref, south_c_ref, below_ref, above_ref, out_ref, step):
    pair, channels, rows, lons = prior_ref.shape
    zonal, north = zonal_ref[...], north_ref[...]
    z_pos, z_neg = jnp.maximum(zonal, 0.0), jnp.minimum(zonal, 0.0)
    n_pos, n_neg = jnp.maximum(north, 0.0), jnp.minimum(north, 0.0)
    south = south_c_ref[0:1]
    s_pos, s_neg = jnp.maximum(south, 0.0), jnp.minimum(south, 0.0)
    row = lax.broadcasted_iota(jnp.int32, (rows, lons), 0)
    lane = lax.broadcasted_iota(jnp.int32, (pair * rows, 128), 1)
    where = pl.ds(pl.multiple_of(step * pair * rows, pair * rows), pair * rows)

    def advanced(i, c):
        p = prior_ref[i, c]
        east = pltpu.roll(p, lons - 1, 1)
        fe = z_pos * p + z_neg * east
        above = jnp.where(row == rows - 1, above_ref[i * channels + c : i * channels + c + 1, :], pltpu.roll(p, rows - 1, 0))
        fn = n_pos * p + n_neg * above
        face = s_pos * below_ref[i * channels + c : i * channels + c + 1, :] + s_neg * p[0:1]
        fs = jnp.where(row == 0, face, pltpu.roll(fn, 1, 0))
        return p - (fe - pltpu.roll(fe, 1, 1)) - (fn - fs)

    for h in range(channels // 8):
        whole = [
            jnp.concatenate([advanced(i, 8 * h + k) for i in range(pair)], axis=0)
            for k in range(8)
        ]
        for q in range(lons // 128):
            moved = swap_lane_groups([w[:, q * 128 : (q + 1) * 128] for w in whole], lane)
            for s in range(8):
                out_ref[q * 8 + s, where, h * 128 : (h + 1) * 128] = moved[s].astype(jnp.bfloat16)


def gram_kernel(perturb_ref, innovation_ref, variance_ref, count_ref, out_ref):
    t = pl.program_id(0)
    perturb = perturb_ref[0]
    members, slots = perturb.shape
    valid = lax.broadcasted_iota(jnp.int32, (1, slots), 1) < count_ref[t]
    variance = variance_ref[pl.ds(t, 1), :]
    weight = jnp.where(valid, variance, 0.0).astype(jnp.bfloat16)
    drive = jnp.where(valid, variance * innovation_ref[pl.ds(t, 1), :], 0.0).astype(jnp.bfloat16)
    weighted = perturb * weight
    first = lax.broadcasted_iota(jnp.int32, (16, slots), 0) == 0
    extra = jnp.where(first, drive.astype(jnp.float32), 0.0).astype(jnp.bfloat16)
    left = jnp.concatenate([weighted, extra], axis=0)
    both = lax.dot_general(
        left, perturb, (((1,), (1,)), ((), ())), preferred_element_type=jnp.float32
    )
    out_ref[0] = both[: members + 8]


def split(x):
    hi = x.astype(jnp.bfloat16)
    return hi, (x - hi.astype(jnp.float32)).astype(jnp.bfloat16)


def dot(a, b):
    return jnp.dot(a, b, preferred_element_type=jnp.float32)


def analysis_kernel(bands, rows, tile_rows, weights_ref, arrived_ref, out_ref, held):
    step = pl.program_id(0)
    members = weights_ref.shape[1]
    wide = members * rows
    per_band = rows // tile_rows

    @pl.when(step < bands)
    def _():
        pick_row = lax.broadcasted_iota(jnp.int32, (wide, per_band * members), 0)
        pick_col = lax.broadcasted_iota(jnp.int32, (wide, per_band * members), 1)
        row_bits, tile_bits = rows.bit_length() - 1, tile_rows.bit_length() - 1
        source = (((pick_row & (rows - 1)) >> tile_bits) * members) + (pick_row >> row_bits)
        pick = jnp.where(pick_col == source, 1.0, 0.0).astype(jnp.bfloat16)
        spread_row = lax.broadcasted_iota(jnp.int32, (members, wide), 0)
        spread_col = lax.broadcasted_iota(jnp.int32, (members, wide), 1)
        spread = jnp.where((spread_col >> row_bits) == spread_row, 1.0, 0.0).astype(jnp.bfloat16)
        here = lax.broadcasted_iota(jnp.int32, (1, rows, wide), 1)
        there = lax.broadcasted_iota(jnp.int32, (1, rows, wide), 2) & (rows - 1)
        diagonal = here == there
        mine = weights_ref[...].reshape(per_band * members, members)
        fields = arrived_ref[...].reshape(wide, arrived_ref.shape[-1])
        total = None
        for part in split(mine):
            tall = dot(pick, part).astype(jnp.bfloat16)
            full = jnp.where(diagonal, dot(tall, spread).reshape(members, rows, wide), 0.0)
            full = full.reshape(wide, wide).astype(jnp.bfloat16)
            term = dot(full, fields)
            total = term if total is None else total + term
        where = pl.ds(pl.multiple_of(step * rows, rows), rows)
        held[:, where, :] = total.reshape(members, rows, fields.shape[-1])

    @pl.when(step >= bands)
    def _():
        count, channels, strip, lat = out_ref.shape
        for k in range(count):
            j = (step - bands) * count + k
            out_ref[k] = held[j].T.reshape(channels, strip, lat)


def iterate(window, neighbours_ref, localization_ref, current, inverse, weights_ref):
    tiles, members = weights_ref.shape[:2]
    row = lax.broadcasted_iota(jnp.int32, (members, members), 0)
    col = lax.broadcasted_iota(jnp.int32, (members, members), 1)
    identity = jnp.where(row == col, 1.0, 0.0)

    def exact(a, b, dims=((1,), (0,))):
        return lax.dot_general(
            a, b, (dims, ((), ())),
            precision=lax.Precision.HIGHEST, preferred_element_type=jnp.float32,
        )

    scales, drives = [], []
    for t in range(tiles):
        total = None
        for n in range(neighbours_ref.shape[1]):
            term = localization_ref[t, n] * window[neighbours_ref[t, n]]
            total = term if total is None else total + term
        curvature = (members - 1.0) * identity + total[:members]
        scale = jnp.sqrt(jnp.sum(curvature * curvature, keepdims=True))
        scales.append(scale)
        drives.append(total[members:])
        current[t] = curvature / scale
        inverse[t] = identity

    def one(_, carry):
        for t in range(tiles):
            now, inv = current[t], inverse[t]
            middle = 1.5 * identity - 0.5 * exact(inv, now)
            current[t] = exact(now, middle)
            inverse[t] = exact(middle, inv)
        return carry

    lax.fori_loop(0, NS_ITERS, one, 0)
    for t in range(tiles):
        inv = inverse[t]
        half = exact(drives[t], inv, ((1,), (1,)))
        shift = exact(half, inv, ((1,), (1,))) / scales[t]
        turned = jnp.sqrt((members - 1.0) / scales[t]) * inv.T + shift[0:1]
        weights_ref[t] = 1.0 / members + turned - jnp.mean(turned, axis=1, keepdims=True)


def transport_kernel(
    prior_ref, zonal_ref, north_ref, south_c_ref, below_ref, above_ref, gram_ref,
    neighbours_ref, localization_ref, got_ref, weights_ref,
    sent, window, current, inverse,
    own_sem, gram_own_sem, send_sems, recv_sems, gram_send_sems, gram_recv_sems,
):
    step, steps = pl.program_id(0), pl.num_programs(0)
    lat_count = lax.axis_size("lat")
    count = lax.axis_size("mem") * lat_count
    me = lax.axis_index("mem") * lat_count + lax.axis_index("lat")
    tiles = gram_ref.shape[0]
    chunks = send_sems.shape[0]
    per_chunk = steps // chunks
    chunk_rows = sent.shape[1] // chunks
    barrier = pltpu.get_barrier_semaphore()

    def place(d):
        return {"mem": d // lat_count, "lat": d % lat_count}

    def sending(chunk, k):
        to = (me + k) % count
        rows = pl.ds(pl.multiple_of(chunk * chunk_rows, chunk_rows), chunk_rows)
        return pltpu.make_async_remote_copy(
            src_ref=sent.at[to, rows],
            dst_ref=got_ref.at[me, rows],
            send_sem=send_sems.at[chunk, k],
            recv_sem=recv_sems.at[chunk, k],
            device_id=place(to),
            device_id_type=pl.DeviceIdType.MESH,
        )

    def arriving(chunk, k):
        origin = (me - k + count) % count
        rows = pl.ds(pl.multiple_of(chunk * chunk_rows, chunk_rows), chunk_rows)
        return pltpu.make_async_remote_copy(
            src_ref=sent.at[origin, rows],
            dst_ref=got_ref.at[origin, rows],
            send_sem=send_sems.at[chunk, k],
            recv_sem=recv_sems.at[chunk, k],
            device_id=place(origin),
            device_id_type=pl.DeviceIdType.MESH,
        )

    def gram_copy(side):
        to = (me + 1) % count if side == 0 else (me - 1 + count) % count
        return pltpu.make_async_remote_copy(
            src_ref=gram_ref,
            dst_ref=window.at[pl.ds(2 * tiles * side, tiles)],
            send_sem=gram_send_sems.at[side],
            recv_sem=gram_recv_sems.at[side],
            device_id=place(to),
            device_id_type=pl.DeviceIdType.MESH,
        )

    gram_own = pltpu.make_async_copy(gram_ref, window.at[pl.ds(tiles, tiles)], gram_own_sem)
    own = pltpu.make_async_copy(sent.at[me], got_ref.at[me], own_sem)

    @pl.when(step == 0)
    def _():
        def greet(k, carry):
            pl.semaphore_signal(
                barrier, inc=1, device_id=place((me + k) % count),
                device_id_type=pl.DeviceIdType.MESH,
            )
            return carry

        lax.fori_loop(1, count, greet, 0)
        pl.semaphore_wait(barrier, count - 1)
        gram_copy(0).start()
        gram_copy(1).start()
        gram_own.start()

    advance(
        prior_ref, zonal_ref, north_ref, south_c_ref, below_ref, above_ref, sent, step
    )

    @pl.when(step % per_chunk == per_chunk - 1)
    def _():
        def begin(k, carry):
            sending(step // per_chunk, k).start()
            return carry

        lax.fori_loop(1, count, begin, 0)

    @pl.when(step == steps - 1)
    def _():
        own.start()
        gram_own.wait()
        gram_copy(0).wait()
        gram_copy(1).wait()
        iterate(window, neighbours_ref, localization_ref, current, inverse, weights_ref)

        def finish(i, carry):
            chunk, k = i // (count - 1), i % (count - 1) + 1
            sending(chunk, k).wait_send()
            arriving(chunk, k).wait_recv()
            return carry

        lax.fori_loop(0, chunks * (count - 1), finish, 0)
        own.wait()


def shifted(axis, wrap):
    size = lax.axis_size(axis)
    up = [(i, (i + 1) % size) for i in range(size if wrap else size - 1)]
    down = [(j, i) for i, j in up]
    return up, down


def fast_device(
    prior_member_stack,
    zonal_stability_ratio,
    meridional_stability_ratio,
    obs_perturb,
    innovation,
    inverse_error_variance,
    obs_count,
    neighbours,
    localization,
):
    members_dev, channels, row_count, lon_count = prior_member_stack.shape
    mem_count = lax.axis_size("mem")
    lat_count = lax.axis_size("lat")
    devices = mem_count * lat_count
    strip = lon_count // devices
    members = members_dev * mem_count
    lat_total = row_count * lat_count
    tiles, slots = innovation.shape
    tile_rows = lat_total // tiles
    params = pltpu.CompilerParams(vmem_limit_bytes=VMEM_BYTES)

    up, down = shifted("lat", False)
    halo = members_dev * channels
    edges = (
        jnp.concatenate(
            [
                prior_member_stack[:, :, row_count - 1, :].reshape(halo, lon_count),
                jnp.broadcast_to(meridional_stability_ratio[row_count - 1 :], (8, lon_count)),
            ]
        ),
        prior_member_stack[:, :, 0, :].reshape(halo, lon_count),
    )
    *edges, obs_count = lax.optimization_barrier((*edges, obs_count))
    below = lax.ppermute(edges[0], "lat", up)
    above = lax.ppermute(edges[1], "lat", down)

    gram = pl.pallas_call(
        gram_kernel,
        grid=(tiles,),
        out_shape=jax.ShapeDtypeStruct((tiles, members + 8, members), jnp.float32),
        in_specs=[
            pl.BlockSpec((1, members, slots), lambda t: (t, 0, 0)),
            pl.BlockSpec((tiles, slots), lambda t: (0, 0)),
            pl.BlockSpec((tiles, slots), lambda t: (0, 0)),
            pl.BlockSpec(memory_space=pltpu.SMEM),
        ],
        out_specs=pl.BlockSpec((1, members + 8, members), lambda t: (t, 0, 0)),
        compiler_params=params,
        cost_estimate=pl.CostEstimate(
            flops=4 * obs_perturb.size * members, bytes_accessed=4 * obs_perturb.size, transcendentals=0
        ),
        name="gram",
    )(obs_perturb, innovation, inverse_error_variance, obs_count)

    pair, chunks = 2, 4
    wire = (devices, members_dev * row_count, channels * strip)
    square = (tiles, members, members)
    arrived, folded = pl.pallas_call(
        transport_kernel,
        grid=(members_dev // pair,),
        out_shape=(
            jax.ShapeDtypeStruct(wire, jnp.bfloat16),
            jax.ShapeDtypeStruct(square, jnp.float32),
        ),
        in_specs=[
            pl.BlockSpec((pair, channels, row_count, lon_count), lambda g: (g, 0, 0, 0)),
            pl.BlockSpec((row_count, lon_count), lambda g: (0, 0)),
            pl.BlockSpec((row_count, lon_count), lambda g: (0, 0)),
            pl.BlockSpec((8, lon_count), lambda g: (halo // 8, 0)),
            pl.BlockSpec((pair * channels, lon_count), lambda g: (g, 0)),
            pl.BlockSpec((pair * channels, lon_count), lambda g: (g, 0)),
            pl.BlockSpec(memory_space=pltpu.VMEM),
            pl.BlockSpec(memory_space=pltpu.SMEM),
            pl.BlockSpec(memory_space=pltpu.SMEM),
        ],
        out_specs=(
            pl.BlockSpec(memory_space=pl.ANY),
            pl.BlockSpec(square, lambda g: (0, 0, 0)),
        ),
        scratch_shapes=[
            pltpu.VMEM(wire, jnp.bfloat16),
            pltpu.VMEM((3 * tiles, members + 8, members), jnp.float32),
            pltpu.VMEM(square, jnp.float32),
            pltpu.VMEM(square, jnp.float32),
            pltpu.SemaphoreType.DMA(()),
            pltpu.SemaphoreType.DMA(()),
            pltpu.SemaphoreType.DMA((chunks, devices)),
            pltpu.SemaphoreType.DMA((chunks, devices)),
            pltpu.SemaphoreType.DMA((2,)),
            pltpu.SemaphoreType.DMA((2,)),
        ],
        compiler_params=pltpu.CompilerParams(
            collective_id=0, has_side_effects=True, vmem_limit_bytes=VMEM_BYTES
        ),
        name="transport",
    )(
        prior_member_stack,
        zonal_stability_ratio,
        meridional_stability_ratio,
        below,
        below,
        above,
        gram,
        neighbours,
        localization,
    )

    per_band = row_count // tile_rows
    j_block = 8
    j_steps = members // j_block
    last = lat_count - 1
    return pl.pallas_call(
        lambda *refs: analysis_kernel(lat_count, row_count, tile_rows, *refs),
        grid=(lat_count + j_steps,),
        out_shape=jax.ShapeDtypeStruct((members, channels, strip, lat_total), jnp.float32),
        in_specs=[
            pl.BlockSpec((per_band, members, members), lambda s: (jnp.minimum(s, last), 0, 0)),
            pl.BlockSpec(
                (mem_count, 1, members_dev * row_count, channels * strip),
                lambda s: (0, jnp.minimum(s, last), 0, 0),
            ),
        ],
        out_specs=pl.BlockSpec(
            (j_block, channels, strip, lat_total),
            lambda s: (jnp.maximum(s - lat_count, 0), 0, 0, 0),
        ),
        scratch_shapes=[pltpu.VMEM((members, lat_total, channels * strip), jnp.float32)],
        compiler_params=params,
        name="analysis",
    )(folded, arrived.reshape(mem_count, lat_count, members_dev * row_count, channels * strip))


def per_device(prior_member_stack, *rest):
    members_dev, channels, row_count, lon_count = prior_member_stack.shape
    lat_count = lax.axis_size("lat")
    devices = lax.axis_size("mem") * lat_count
    tiles = rest[3].shape[0]
    tile_rows = row_count * lat_count // tiles
    fits = (
        lon_count == 16 * devices
        and channels % 8 == 0
        and row_count == 8
        and tile_rows in (1, 2, 4, 8)
        and members_dev % 8 == 0
    )
    return (fast_device if fits else general_device)(prior_member_stack, *rest)


def solution(mesh):
    in_specs = (
        P("mem", None, "lat", None),
        P("lat", None),
        P("lat", None),
        P(("mem", "lat"), None, None),
        P(("mem", "lat"), None),
        P(("mem", "lat"), None),
        P(("mem", "lat")),
        P(("mem", "lat"), None),
        P(("mem", "lat"), None),
    )
    out_specs = P(None, None, ("mem", "lat"), None)
    return jax.shard_map(
        per_device, mesh=mesh, in_specs=in_specs, out_specs=out_specs, check_vma=False
    )
```

```python
import jax
import jax.numpy as jnp
from jax import lax
from jax.experimental import pallas as pl
from jax.experimental.pallas import tpu as pltpu
from jax.sharding import PartitionSpec as P

NS_ITERS = 5
VMEM_BYTES = 48 * 1024 * 1024


def extended(x, sides, width, wrap):
    for axis, dim in sides:
        size, length = (lax.axis_size(axis), x.shape[dim])
        up = [(i, (i + 1) % size) for i in range(size if wrap else size - 1)]
        down = [(j, i) for i, j in up]
        last = lax.slice_in_dim(x, length - width, length, axis=dim)
        leading = lax.slice_in_dim(x, 0, width, axis=dim)
        before = lax.ppermute(last, axis, up)
        after = lax.ppermute(leading, axis, down)
        x = jnp.concatenate([before, x, after], axis=dim)
    return x


def tile_terms(perturb, weight, drive):
    weighted = (perturb.astype(jnp.float32) * weight.astype(jnp.float32)[:, None, :]).astype(
        jnp.bfloat16
    )
    gram_matrix = jnp.einsum("tko,tlo->tkl", weighted, perturb, preferred_element_type=jnp.float32)
    drive_vector = jnp.einsum("tko,to->tk", perturb, drive, preferred_element_type=jnp.float32)
    return (gram_matrix, drive_vector)


def transform_weights(curvature, drive_total, members):
    frob_scale = jnp.sqrt(jnp.sum(curvature * curvature, axis=(1, 2)))
    identity = jnp.eye(members, dtype=jnp.float32)[None]
    current = curvature / frob_scale[:, None, None]
    inverse = jnp.broadcast_to(identity, curvature.shape)
    for _ in range(NS_ITERS):
        middle = 1.5 * identity - 0.5 * jnp.einsum(
            "tij,tjk->tik", inverse, current, precision=lax.Precision.HIGHEST
        )
        current = jnp.einsum("tij,tjk->tik", current, middle, precision=lax.Precision.HIGHEST)
        inverse = jnp.einsum("tij,tjk->tik", middle, inverse, precision=lax.Precision.HIGHEST)
    spread_part = jnp.sqrt((members - 1.0) / frob_scale)[:, None, None] * inverse
    half_step = jnp.einsum("tij,tj->ti", inverse, drive_total, precision=lax.Precision.HIGHEST)
    ensemble_mean_portion = (
        jnp.einsum("tij,tj->ti", inverse, half_step, precision=lax.Precision.HIGHEST)
        / frob_scale[:, None]
    )
    return spread_part + ensemble_mean_portion[:, :, None]


def general_device(
    prior_member_stack,
    zonal_stability_ratio,
    meridional_stability_ratio,
    obs_perturb,
    innovation,
    inverse_error_variance,
    obs_count,
    neighbours,
    localization,
):
    members_dev, channels, row_count, lon_count = prior_member_stack.shape
    mem_count = lax.axis_size("mem")
    lat_count = lax.axis_size("lat")
    lon_strip = lon_count // (mem_count * lat_count)
    members = members_dev * mem_count
    lat_total = row_count * lat_count
    east_neighbour = jnp.roll(prior_member_stack, -1, axis=-1)
    eastward_flux = (
        jnp.maximum(zonal_stability_ratio, 0.0) * prior_member_stack
        + jnp.minimum(zonal_stability_ratio, 0.0) * east_neighbour
    )
    divergence_x = eastward_flux - jnp.roll(eastward_flux, 1, axis=-1)
    stacked = jnp.concatenate(
        [
            prior_member_stack.reshape(members_dev * channels, row_count, lon_count),
            meridional_stability_ratio[None],
        ],
        axis=0,
    )
    padded = extended(stacked, (("lat", 1),), 1, False)
    fields_ext = padded[:-1].reshape(members_dev, channels, row_count + 2, lon_count)
    north_ext = padded[-1, :-1]
    flux_north = (
        jnp.maximum(north_ext, 0.0) * fields_ext[:, :, : row_count + 1]
        + jnp.minimum(north_ext, 0.0) * fields_ext[:, :, 1:]
    )
    transported_quantities = (
        prior_member_stack - divergence_x - (flux_north[:, :, 1:] - flux_north[:, :, :-1])
    )
    rows_last = jnp.swapaxes(transported_quantities, 2, 3)
    moved = rows_last.reshape(1, members_dev, channels, lon_count, row_count)
    arrived = lax.all_to_all(moved, ("mem", "lat"), split_axis=3, concat_axis=0, tiled=True)
    arrived = arrived.reshape(mem_count, lat_count, members_dev, channels, lon_strip, row_count)
    arrived = jnp.transpose(arrived, (0, 2, 3, 4, 1, 5)).reshape(
        members, channels, lon_strip, lat_total
    )
    blocks_per_processor, obs_cap = innovation.shape
    neigh_count = neighbours.shape[1]
    window_tiles = 3 * blocks_per_processor
    is_valid = (
        lax.broadcasted_iota(jnp.int32, (blocks_per_processor, obs_cap), 1) < obs_count[:, None]
    )
    obs_weight = jnp.where(is_valid, inverse_error_variance, 0.0).astype(jnp.bfloat16)
    obs_drive = jnp.where(is_valid, inverse_error_variance * innovation, 0.0).astype(jnp.bfloat16)
    window_slots = lax.broadcasted_iota(jnp.int32, (blocks_per_processor, window_tiles), 1)
    combine = jnp.zeros((blocks_per_processor, window_tiles), jnp.float32)
    for slot_index in range(neigh_count):
        combine = combine + jnp.where(
            neighbours[:, slot_index, None] == window_slots, localization[:, slot_index, None], 0.0
        )
    observed = jnp.concatenate([obs_perturb, obs_weight[:, None, :], obs_drive[:, None, :]], axis=1)
    received = extended(observed, ((("mem", "lat"), 0),), blocks_per_processor, True)
    gram_matrix, drive_vector = tile_terms(
        received[:, :members], received[:, members], received[:, members + 1]
    )
    window = jnp.concatenate([gram_matrix, drive_vector[:, None, :]], axis=1)
    gathered = jnp.einsum("ts,skl->tkl", combine, window, precision=lax.Precision.HIGHEST)
    curvature = (members - 1.0) * jnp.eye(members, dtype=jnp.float32)[None] + gathered[:, :members]
    drive_total = gathered[:, members]
    weights = transform_weights(curvature, drive_total, members)
    grid = arrived.reshape(
        members, channels, lon_strip, blocks_per_processor, lat_total // blocks_per_processor
    )
    member_mean = jnp.mean(grid, axis=0)
    anomaly = grid - member_mean
    update = jnp.einsum("icxtr,tij->jcxtr", anomaly, weights, precision=lax.Precision.HIGHEST)
    return (member_mean + update).reshape(members, channels, lon_strip, lat_total)


def swap_lane_groups(blocks, lane):
    blocks = list(blocks)
    count = len(blocks)
    width = lane.shape[1] // count
    bit = 1
    while bit < count:
        keep = (lane // width) & bit == 0
        for k in range(count):
            if k & bit == 0:
                a, b = blocks[k], blocks[k | bit]
                blocks[k] = jnp.where(keep, a, pltpu.roll(b, bit * width, 1))
                blocks[k | bit] = jnp.where(keep, pltpu.roll(a, lane.shape[1] - bit * width, 1), b)
        bit *= 2
    return blocks


def advance(prior_ref, zonal_ref, north_ref, south_c_ref, below_ref, above_ref, out_ref, step):
    pair, channels, rows, lons = prior_ref.shape
    zonal, north = zonal_ref[...], north_ref[...]
    z_pos, z_neg = jnp.maximum(zonal, 0.0), jnp.minimum(zonal, 0.0)
    n_pos, n_neg = jnp.maximum(north, 0.0), jnp.minimum(north, 0.0)
    south = south_c_ref[0:1]
    s_pos, s_neg = jnp.maximum(south, 0.0), jnp.minimum(south, 0.0)
    row = lax.broadcasted_iota(jnp.int32, (rows, lons), 0)
    lane = lax.broadcasted_iota(jnp.int32, (pair * rows, 128), 1)
    where = pl.ds(pl.multiple_of(step * pair * rows, pair * rows), pair * rows)

    def advanced(i, c):
        p = prior_ref[i, c]
        east = pltpu.roll(p, lons - 1, 1)
        fe = z_pos * p + z_neg * east
        above = jnp.where(row == rows - 1, above_ref[i * channels + c : i * channels + c + 1, :], pltpu.roll(p, rows - 1, 0))
        fn = n_pos * p + n_neg * above
        face = s_pos * below_ref[i * channels + c : i * channels + c + 1, :] + s_neg * p[0:1]
        fs = jnp.where(row == 0, face, pltpu.roll(fn, 1, 0))
        return p - (fe - pltpu.roll(fe, 1, 1)) - (fn - fs)

    for h in range(channels // 8):
        whole = [
            jnp.concatenate([advanced(i, 8 * h + k) for i in range(pair)], axis=0)
            for k in range(8)
        ]
        for q in range(lons // 128):
            moved = swap_lane_groups([w[:, q * 128 : (q + 1) * 128] for w in whole], lane)
            for s in range(8):
                out_ref[q * 8 + s, where, h * 128 : (h + 1) * 128] = moved[s].astype(jnp.bfloat16)


def gram_kernel(perturb_ref, innovation_ref, variance_ref, count_ref, out_ref):
    t = pl.program_id(0)
    perturb = perturb_ref[0]
    members, slots = perturb.shape
    valid = lax.broadcasted_iota(jnp.int32, (1, slots), 1) < count_ref[t]
    variance = variance_ref[pl.ds(t, 1), :]
    weight = jnp.where(valid, variance, 0.0).astype(jnp.bfloat16)
    drive = jnp.where(valid, variance * innovation_ref[pl.ds(t, 1), :], 0.0).astype(jnp.bfloat16)
    weighted = perturb * weight
    first = lax.broadcasted_iota(jnp.int32, (16, slots), 0) == 0
    extra = jnp.where(first, drive.astype(jnp.float32), 0.0).astype(jnp.bfloat16)
    left = jnp.concatenate([weighted, extra], axis=0)
    both = lax.dot_general(
        left, perturb, (((1,), (1,)), ((), ())), preferred_element_type=jnp.float32
    )
    out_ref[0] = both[: members + 8]


def split(x):
    hi = x.astype(jnp.bfloat16)
    return hi, (x - hi.astype(jnp.float32)).astype(jnp.bfloat16)


def dot(a, b):
    return jnp.dot(a, b, preferred_element_type=jnp.float32)


def analysis_kernel(bands, rows, tile_rows, weights_ref, arrived_ref, out_ref, held):
    step = pl.program_id(0)
    members = weights_ref.shape[1]
    wide = members * rows
    per_band = rows // tile_rows

    @pl.when(step < bands)
    def _():
        row_bits = rows.bit_length() - 1
        spread_row = lax.broadcasted_iota(jnp.int32, (members, wide), 0)
        spread_col = lax.broadcasted_iota(jnp.int32, (members, wide), 1)
        spread = jnp.where((spread_col >> row_bits) == spread_row, 1.0, 0.0).astype(jnp.bfloat16)
        here = lax.broadcasted_iota(jnp.int32, (1, rows, wide), 1)
        there = lax.broadcasted_iota(jnp.int32, (1, rows, wide), 2) & (rows - 1)
        diagonal = here == there
        mine = weights_ref[...].reshape(per_band * members, members)
        fields = arrived_ref[...].reshape(wide, arrived_ref.shape[-1])
        total = None
        sub = lax.broadcasted_iota(jnp.int32, (1, rows, wide), 1)
        for part in split(mine):
            tall = dot(part, spread)
            full = None
            for t in range(per_band):
                piece = tall[t * members : (t + 1) * members].reshape(members, 1, wide)
                own = diagonal & (sub >= t * tile_rows) & (sub < (t + 1) * tile_rows)
                full = jnp.where(own, piece, 0.0 if full is None else full)
            full = full.reshape(wide, wide).astype(jnp.bfloat16)
            term = dot(full, fields)
            total = term if total is None else total + term
        where = pl.ds(pl.multiple_of(step * rows, rows), rows)
        held[:, where, :] = total.reshape(members, rows, fields.shape[-1])

    @pl.when(step >= bands)
    def _():
        count, channels, strip, lat = out_ref.shape
        for k in range(count):
            j = (step - bands) * count + k
            out_ref[k] = held[j].T.reshape(channels, strip, lat)


def iterate(window, neighbours_ref, localization_ref, current, inverse, weights_ref):
    tiles, members = weights_ref.shape[:2]
    row = lax.broadcasted_iota(jnp.int32, (members, members), 0)
    col = lax.broadcasted_iota(jnp.int32, (members, members), 1)
    identity = jnp.where(row == col, 1.0, 0.0)

    def exact(a, b, dims=((1,), (0,))):
        return lax.dot_general(
            a, b, (dims, ((), ())),
            precision=lax.Precision.HIGHEST, preferred_element_type=jnp.float32,
        )

    def product(a, b):
        a_hi, a_lo = split(a)
        b_hi, b_lo = split(b)
        return dot(
            jnp.concatenate([a_hi, a_hi, a_lo], axis=1),
            jnp.concatenate([b_hi, b_lo, b_hi], axis=0),
        )

    scales, drives = [], []
    for t in range(tiles):
        total = None
        for n in range(neighbours_ref.shape[1]):
            term = localization_ref[t, n] * window[neighbours_ref[t, n]]
            total = term if total is None else total + term
        curvature = (members - 1.0) * identity + total[:members]
        scale = jnp.sqrt(jnp.sum(curvature * curvature, keepdims=True))
        scales.append(scale)
        drives.append(total[members:])
        current[t] = curvature / scale
        inverse[t] = identity

    def one(_, carry):
        for t in range(tiles):
            now, inv = current[t], inverse[t]
            middle = 1.5 * identity - 0.5 * product(inv, now)
            current[t] = product(now, middle)
            inverse[t] = product(middle, inv)
        return carry

    lax.fori_loop(0, NS_ITERS, one, 0)
    for t in range(tiles):
        inv = inverse[t]
        half = exact(drives[t], inv, ((1,), (1,)))
        shift = exact(half, inv, ((1,), (1,))) / scales[t]
        turned = jnp.sqrt((members - 1.0) / scales[t]) * inv.T + shift[0:1]
        weights_ref[t] = 1.0 / members + turned - jnp.mean(turned, axis=1, keepdims=True)


def transport_kernel(
    prior_ref, zonal_ref, north_ref, south_c_ref, below_ref, above_ref, gram_ref,
    neighbours_ref, localization_ref, got_ref, weights_ref,
    sent, window, current, inverse,
    own_sem, gram_own_sem, send_sems, recv_sems, gram_send_sems, gram_recv_sems,
):
    step, steps = pl.program_id(0), pl.num_programs(0)
    lat_count = lax.axis_size("lat")
    count = lax.axis_size("mem") * lat_count
    me = lax.axis_index("mem") * lat_count + lax.axis_index("lat")
    tiles = gram_ref.shape[0]
    chunks = send_sems.shape[0]
    per_chunk = steps // chunks
    chunk_rows = sent.shape[1] // chunks
    barrier = pltpu.get_barrier_semaphore()

    def place(d):
        return {"mem": d // lat_count, "lat": d % lat_count}

    def sending(chunk, k):
        to = (me + k) % count
        rows = pl.ds(pl.multiple_of(chunk * chunk_rows, chunk_rows), chunk_rows)
        return pltpu.make_async_remote_copy(
            src_ref=sent.at[to, rows],
            dst_ref=got_ref.at[me, rows],
            send_sem=send_sems.at[chunk, k],
            recv_sem=recv_sems.at[chunk, k],
            device_id=place(to),
            device_id_type=pl.DeviceIdType.MESH,
        )

    def arriving(chunk, k):
        origin = (me - k + count) % count
        rows = pl.ds(pl.multiple_of(chunk * chunk_rows, chunk_rows), chunk_rows)
        return pltpu.make_async_remote_copy(
            src_ref=sent.at[origin, rows],
            dst_ref=got_ref.at[origin, rows],
            send_sem=send_sems.at[chunk, k],
            recv_sem=recv_sems.at[chunk, k],
            device_id=place(origin),
            device_id_type=pl.DeviceIdType.MESH,
        )

    def gram_copy(side):
        to = (me + 1) % count if side == 0 else (me - 1 + count) % count
        return pltpu.make_async_remote_copy(
            src_ref=gram_ref,
            dst_ref=window.at[pl.ds(2 * tiles * side, tiles)],
            send_sem=gram_send_sems.at[side],
            recv_sem=gram_recv_sems.at[side],
            device_id=place(to),
            device_id_type=pl.DeviceIdType.MESH,
        )

    gram_own = pltpu.make_async_copy(gram_ref, window.at[pl.ds(tiles, tiles)], gram_own_sem)
    own = pltpu.make_async_copy(sent.at[me], got_ref.at[me], own_sem)

    @pl.when(step == 0)
    def _():
        def greet(k, carry):
            pl.semaphore_signal(
                barrier, inc=1, device_id=place((me + k) % count),
                device_id_type=pl.DeviceIdType.MESH,
            )
            return carry

        lax.fori_loop(1, count, greet, 0)
        pl.semaphore_wait(barrier, count - 1)
        gram_copy(0).start()
        gram_copy(1).start()
        gram_own.start()

    advance(
        prior_ref, zonal_ref, north_ref, south_c_ref, below_ref, above_ref, sent, step
    )

    @pl.when(step % per_chunk == per_chunk - 1)
    def _():
        def begin(k, carry):
            sending(step // per_chunk, k).start()
            return carry

        lax.fori_loop(1, count, begin, 0)

    @pl.when(step == steps - 1)
    def _():
        own.start()
        gram_own.wait()
        gram_copy(0).wait()
        gram_copy(1).wait()
        iterate(window, neighbours_ref, localization_ref, current, inverse, weights_ref)

        def finish(i, carry):
            chunk, k = i // (count - 1), i % (count - 1) + 1
            sending(chunk, k).wait_send()
            arriving(chunk, k).wait_recv()
            return carry

        lax.fori_loop(0, chunks * (count - 1), finish, 0)
        own.wait()


def shifted(axis, wrap):
    size = lax.axis_size(axis)
    up = [(i, (i + 1) % size) for i in range(size if wrap else size - 1)]
    down = [(j, i) for i, j in up]
    return up, down


def fast_device(
    prior_member_stack,
    zonal_stability_ratio,
    meridional_stability_ratio,
    obs_perturb,
    innovation,
    inverse_error_variance,
    obs_count,
    neighbours,
    localization,
):
    members_dev, channels, row_count, lon_count = prior_member_stack.shape
    mem_count = lax.axis_size("mem")
    lat_count = lax.axis_size("lat")
    devices = mem_count * lat_count
    strip = lon_count // devices
    members = members_dev * mem_count
    lat_total = row_count * lat_count
    tiles, slots = innovation.shape
    tile_rows = lat_total // tiles
    params = pltpu.CompilerParams(vmem_limit_bytes=VMEM_BYTES)

    up, down = shifted("lat", False)
    halo = members_dev * channels
    edges = (
        jnp.concatenate(
            [
                prior_member_stack[:, :, row_count - 1, :].reshape(halo, lon_count),
                jnp.broadcast_to(meridional_stability_ratio[row_count - 1 :], (8, lon_count)),
            ]
        ),
        prior_member_stack[:, :, 0, :].reshape(halo, lon_count),
    )
    *edges, obs_count = lax.optimization_barrier((*edges, obs_count))
    below = lax.ppermute(edges[0], "lat", up)
    above = lax.ppermute(edges[1], "lat", down)

    gram = pl.pallas_call(
        gram_kernel,
        grid=(tiles,),
        out_shape=jax.ShapeDtypeStruct((tiles, members + 8, members), jnp.float32),
        in_specs=[
            pl.BlockSpec((1, members, slots), lambda t: (t, 0, 0)),
            pl.BlockSpec((tiles, slots), lambda t: (0, 0)),
            pl.BlockSpec((tiles, slots), lambda t: (0, 0)),
            pl.BlockSpec(memory_space=pltpu.SMEM),
        ],
        out_specs=pl.BlockSpec((1, members + 8, members), lambda t: (t, 0, 0)),
        compiler_params=params,
        cost_estimate=pl.CostEstimate(
            flops=4 * obs_perturb.size * members, bytes_accessed=4 * obs_perturb.size, transcendentals=0
        ),
        name="gram",
    )(obs_perturb, innovation, inverse_error_variance, obs_count)

    pair, chunks = 2, 4
    wire = (devices, members_dev * row_count, channels * strip)
    square = (tiles, members, members)
    arrived, folded = pl.pallas_call(
        transport_kernel,
        grid=(members_dev // pair,),
        out_shape=(
            jax.ShapeDtypeStruct(wire, jnp.bfloat16),
            jax.ShapeDtypeStruct(square, jnp.float32),
        ),
        in_specs=[
            pl.BlockSpec((pair, channels, row_count, lon_count), lambda g: (g, 0, 0, 0)),
            pl.BlockSpec((row_count, lon_count), lambda g: (0, 0)),
            pl.BlockSpec((row_count, lon_count), lambda g: (0, 0)),
            pl.BlockSpec((8, lon_count), lambda g: (halo // 8, 0)),
            pl.BlockSpec((pair * channels, lon_count), lambda g: (g, 0)),
            pl.BlockSpec((pair * channels, lon_count), lambda g: (g, 0)),
            pl.BlockSpec(memory_space=pltpu.VMEM),
            pl.BlockSpec(memory_space=pltpu.SMEM),
            pl.BlockSpec(memory_space=pltpu.SMEM),
        ],
        out_specs=(
            pl.BlockSpec(memory_space=pl.ANY),
            pl.BlockSpec(square, lambda g: (0, 0, 0)),
        ),
        scratch_shapes=[
            pltpu.VMEM(wire, jnp.bfloat16),
            pltpu.VMEM((3 * tiles, members + 8, members), jnp.float32),
            pltpu.VMEM(square, jnp.float32),
            pltpu.VMEM(square, jnp.float32),
            pltpu.SemaphoreType.DMA(()),
            pltpu.SemaphoreType.DMA(()),
            pltpu.SemaphoreType.DMA((chunks, devices)),
            pltpu.SemaphoreType.DMA((chunks, devices)),
            pltpu.SemaphoreType.DMA((2,)),
            pltpu.SemaphoreType.DMA((2,)),
        ],
        compiler_params=pltpu.CompilerParams(
            collective_id=0, has_side_effects=True, vmem_limit_bytes=VMEM_BYTES
        ),
        name="transport",
    )(
        prior_member_stack,
        zonal_stability_ratio,
        meridional_stability_ratio,
        below,
        below,
        above,
        gram,
        neighbours,
        localization,
    )

    per_band = row_count // tile_rows
    j_block = 8
    j_steps = members // j_block
    last = lat_count - 1
    return pl.pallas_call(
        lambda *refs: analysis_kernel(lat_count, row_count, tile_rows, *refs),
        grid=(lat_count + j_steps,),
        out_shape=jax.ShapeDtypeStruct((members, channels, strip, lat_total), jnp.float32),
        in_specs=[
            pl.BlockSpec((per_band, members, members), lambda s: (jnp.minimum(s, last), 0, 0)),
            pl.BlockSpec(
                (mem_count, 1, members_dev * row_count, channels * strip),
                lambda s: (0, jnp.minimum(s, last), 0, 0),
            ),
        ],
        out_specs=pl.BlockSpec(
            (j_block, channels, strip, lat_total),
            lambda s: (jnp.maximum(s - lat_count, 0), 0, 0, 0),
        ),
        scratch_shapes=[pltpu.VMEM((members, lat_total, channels * strip), jnp.float32)],
        compiler_params=params,
        name="analysis",
    )(folded, arrived.reshape(mem_count, lat_count, members_dev * row_count, channels * strip))


def per_device(prior_member_stack, *rest):
    members_dev, channels, row_count, lon_count = prior_member_stack.shape
    lat_count = lax.axis_size("lat")
    devices = lax.axis_size("mem") * lat_count
    tiles = rest[3].shape[0]
    tile_rows = row_count * lat_count // tiles
    fits = (
        lon_count == 16 * devices
        and channels % 8 == 0
        and row_count == 8
        and tile_rows in (1, 2, 4, 8)
        and members_dev % 8 == 0
    )
    return (fast_device if fits else general_device)(prior_member_stack, *rest)


def solution(mesh):
    in_specs = (
        P("mem", None, "lat", None),
        P("lat", None),
        P("lat", None),
        P(("mem", "lat"), None, None),
        P(("mem", "lat"), None),
        P(("mem", "lat"), None),
        P(("mem", "lat")),
        P(("mem", "lat"), None),
        P(("mem", "lat"), None),
    )
    out_specs = P(None, None, ("mem", "lat"), None)
    return jax.shard_map(
        per_device, mesh=mesh, in_specs=in_specs, out_specs=out_specs, check_vma=False
    )
```

```python
import jax
import jax.numpy as jnp
from jax import lax
from jax.experimental import pallas as pl
from jax.experimental.pallas import tpu as pltpu
from jax.sharding import PartitionSpec as P

NS_ITERS = 5
VMEM_BYTES = 48 * 1024 * 1024


def extended(x, sides, width, wrap):
    for axis, dim in sides:
        size, length = (lax.axis_size(axis), x.shape[dim])
        up = [(i, (i + 1) % size) for i in range(size if wrap else size - 1)]
        down = [(j, i) for i, j in up]
        last = lax.slice_in_dim(x, length - width, length, axis=dim)
        leading = lax.slice_in_dim(x, 0, width, axis=dim)
        before = lax.ppermute(last, axis, up)
        after = lax.ppermute(leading, axis, down)
        x = jnp.concatenate([before, x, after], axis=dim)
    return x


def tile_terms(perturb, weight, drive):
    weighted = (perturb.astype(jnp.float32) * weight.astype(jnp.float32)[:, None, :]).astype(
        jnp.bfloat16
    )
    gram_matrix = jnp.einsum("tko,tlo->tkl", weighted, perturb, preferred_element_type=jnp.float32)
    drive_vector = jnp.einsum("tko,to->tk", perturb, drive, preferred_element_type=jnp.float32)
    return (gram_matrix, drive_vector)


def transform_weights(curvature, drive_total, members):
    frob_scale = jnp.sqrt(jnp.sum(curvature * curvature, axis=(1, 2)))
    identity = jnp.eye(members, dtype=jnp.float32)[None]
    current = curvature / frob_scale[:, None, None]
    inverse = jnp.broadcast_to(identity, curvature.shape)
    for _ in range(NS_ITERS):
        middle = 1.5 * identity - 0.5 * jnp.einsum(
            "tij,tjk->tik", inverse, current, precision=lax.Precision.HIGHEST
        )
        current = jnp.einsum("tij,tjk->tik", current, middle, precision=lax.Precision.HIGHEST)
        inverse = jnp.einsum("tij,tjk->tik", middle, inverse, precision=lax.Precision.HIGHEST)
    spread_part = jnp.sqrt((members - 1.0) / frob_scale)[:, None, None] * inverse
    half_step = jnp.einsum("tij,tj->ti", inverse, drive_total, precision=lax.Precision.HIGHEST)
    ensemble_mean_portion = (
        jnp.einsum("tij,tj->ti", inverse, half_step, precision=lax.Precision.HIGHEST)
        / frob_scale[:, None]
    )
    return spread_part + ensemble_mean_portion[:, :, None]


def general_device(
    prior_member_stack,
    zonal_stability_ratio,
    meridional_stability_ratio,
    obs_perturb,
    innovation,
    inverse_error_variance,
    obs_count,
    neighbours,
    localization,
):
    members_dev, channels, row_count, lon_count = prior_member_stack.shape
    mem_count = lax.axis_size("mem")
    lat_count = lax.axis_size("lat")
    lon_strip = lon_count // (mem_count * lat_count)
    members = members_dev * mem_count
    lat_total = row_count * lat_count
    east_neighbour = jnp.roll(prior_member_stack, -1, axis=-1)
    eastward_flux = (
        jnp.maximum(zonal_stability_ratio, 0.0) * prior_member_stack
        + jnp.minimum(zonal_stability_ratio, 0.0) * east_neighbour
    )
    divergence_x = eastward_flux - jnp.roll(eastward_flux, 1, axis=-1)
    stacked = jnp.concatenate(
        [
            prior_member_stack.reshape(members_dev * channels, row_count, lon_count),
            meridional_stability_ratio[None],
        ],
        axis=0,
    )
    padded = extended(stacked, (("lat", 1),), 1, False)
    fields_ext = padded[:-1].reshape(members_dev, channels, row_count + 2, lon_count)
    north_ext = padded[-1, :-1]
    flux_north = (
        jnp.maximum(north_ext, 0.0) * fields_ext[:, :, : row_count + 1]
        + jnp.minimum(north_ext, 0.0) * fields_ext[:, :, 1:]
    )
    transported_quantities = (
        prior_member_stack - divergence_x - (flux_north[:, :, 1:] - flux_north[:, :, :-1])
    )
    rows_last = jnp.swapaxes(transported_quantities, 2, 3)
    moved = rows_last.reshape(1, members_dev, channels, lon_count, row_count)
    arrived = lax.all_to_all(moved, ("mem", "lat"), split_axis=3, concat_axis=0, tiled=True)
    arrived = arrived.reshape(mem_count, lat_count, members_dev, channels, lon_strip, row_count)
    arrived = jnp.transpose(arrived, (0, 2, 3, 4, 1, 5)).reshape(
        members, channels, lon_strip, lat_total
    )
    blocks_per_processor, obs_cap = innovation.shape
    neigh_count = neighbours.shape[1]
    window_tiles = 3 * blocks_per_processor
    is_valid = (
        lax.broadcasted_iota(jnp.int32, (blocks_per_processor, obs_cap), 1) < obs_count[:, None]
    )
    obs_weight = jnp.where(is_valid, inverse_error_variance, 0.0).astype(jnp.bfloat16)
    obs_drive = jnp.where(is_valid, inverse_error_variance * innovation, 0.0).astype(jnp.bfloat16)
    window_slots = lax.broadcasted_iota(jnp.int32, (blocks_per_processor, window_tiles), 1)
    combine = jnp.zeros((blocks_per_processor, window_tiles), jnp.float32)
    for slot_index in range(neigh_count):
        combine = combine + jnp.where(
            neighbours[:, slot_index, None] == window_slots, localization[:, slot_index, None], 0.0
        )
    observed = jnp.concatenate([obs_perturb, obs_weight[:, None, :], obs_drive[:, None, :]], axis=1)
    received = extended(observed, ((("mem", "lat"), 0),), blocks_per_processor, True)
    gram_matrix, drive_vector = tile_terms(
        received[:, :members], received[:, members], received[:, members + 1]
    )
    window = jnp.concatenate([gram_matrix, drive_vector[:, None, :]], axis=1)
    gathered = jnp.einsum("ts,skl->tkl", combine, window, precision=lax.Precision.HIGHEST)
    curvature = (members - 1.0) * jnp.eye(members, dtype=jnp.float32)[None] + gathered[:, :members]
    drive_total = gathered[:, members]
    weights = transform_weights(curvature, drive_total, members)
    grid = arrived.reshape(
        members, channels, lon_strip, blocks_per_processor, lat_total // blocks_per_processor
    )
    member_mean = jnp.mean(grid, axis=0)
    anomaly = grid - member_mean
    update = jnp.einsum("icxtr,tij->jcxtr", anomaly, weights, precision=lax.Precision.HIGHEST)
    return (member_mean + update).reshape(members, channels, lon_strip, lat_total)


def swap_lane_groups(blocks, lane):
    blocks = list(blocks)
    count = len(blocks)
    width = lane.shape[1] // count
    bit = 1
    while bit < count:
        keep = (lane // width) & bit == 0
        for k in range(count):
            if k & bit == 0:
                a, b = blocks[k], blocks[k | bit]
                blocks[k] = jnp.where(keep, a, pltpu.roll(b, bit * width, 1))
                blocks[k | bit] = jnp.where(keep, pltpu.roll(a, lane.shape[1] - bit * width, 1), b)
        bit *= 2
    return blocks


def advance(prior_ref, zonal_ref, north_ref, south_c_ref, below_ref, above_ref, out_ref, step):
    pair, channels, rows, lons = prior_ref.shape
    zonal, north = zonal_ref[...], north_ref[...]
    z_pos, z_neg = jnp.maximum(zonal, 0.0), jnp.minimum(zonal, 0.0)
    n_pos, n_neg = jnp.maximum(north, 0.0), jnp.minimum(north, 0.0)
    south = south_c_ref[0:1]
    s_pos, s_neg = jnp.maximum(south, 0.0), jnp.minimum(south, 0.0)
    row = lax.broadcasted_iota(jnp.int32, (rows, lons), 0)
    lane = lax.broadcasted_iota(jnp.int32, (pair * rows, 128), 1)
    where = pl.ds(pl.multiple_of(step * pair * rows, pair * rows), pair * rows)

    def advanced(i, c):
        p = prior_ref[i, c]
        east = pltpu.roll(p, lons - 1, 1)
        fe = z_pos * p + z_neg * east
        above = jnp.where(row == rows - 1, above_ref[i * channels + c : i * channels + c + 1, :], pltpu.roll(p, rows - 1, 0))
        fn = n_pos * p + n_neg * above
        face = s_pos * below_ref[i * channels + c : i * channels + c + 1, :] + s_neg * p[0:1]
        fs = jnp.where(row == 0, face, pltpu.roll(fn, 1, 0))
        return p - (fe - pltpu.roll(fe, 1, 1)) - (fn - fs)

    for h in range(channels // 8):
        whole = [
            jnp.concatenate([advanced(i, 8 * h + k) for i in range(pair)], axis=0)
            for k in range(8)
        ]
        for q in range(lons // 128):
            moved = swap_lane_groups([w[:, q * 128 : (q + 1) * 128] for w in whole], lane)
            for s in range(8):
                out_ref[q * 8 + s, where, h * 128 : (h + 1) * 128] = moved[s].astype(jnp.bfloat16)


def gram_kernel(perturb_ref, innovation_ref, variance_ref, count_ref, out_ref):
    t = pl.program_id(0)
    perturb = perturb_ref[0]
    members, slots = perturb.shape
    valid = lax.broadcasted_iota(jnp.int32, (1, slots), 1) < count_ref[t]
    variance = variance_ref[pl.ds(t, 1), :]
    weight = jnp.where(valid, variance, 0.0).astype(jnp.bfloat16)
    drive = jnp.where(valid, variance * innovation_ref[pl.ds(t, 1), :], 0.0).astype(jnp.bfloat16)
    weighted = perturb * weight
    first = lax.broadcasted_iota(jnp.int32, (16, slots), 0) == 0
    extra = jnp.where(first, drive.astype(jnp.float32), 0.0).astype(jnp.bfloat16)
    left = jnp.concatenate([weighted, extra], axis=0)
    both = lax.dot_general(
        left, perturb, (((1,), (1,)), ((), ())), preferred_element_type=jnp.float32
    )
    out_ref[0] = both[: members + 8]


def split(x):
    hi = x.astype(jnp.bfloat16)
    return hi, (x - hi.astype(jnp.float32)).astype(jnp.bfloat16)


def dot(a, b):
    return jnp.dot(a, b, preferred_element_type=jnp.float32)


def analysis_kernel(bands, rows, tile_rows, weights_ref, arrived_ref, out_ref, held):
    step = pl.program_id(0)
    members = weights_ref.shape[1]
    wide = members * rows
    per_band = rows // tile_rows

    @pl.when(step < bands)
    def _():
        row_bits = rows.bit_length() - 1
        spread_row = lax.broadcasted_iota(jnp.int32, (members, wide), 0)
        spread_col = lax.broadcasted_iota(jnp.int32, (members, wide), 1)
        spread = jnp.where((spread_col >> row_bits) == spread_row, 1.0, 0.0).astype(jnp.bfloat16)
        here = lax.broadcasted_iota(jnp.int32, (1, rows, wide), 1)
        there = lax.broadcasted_iota(jnp.int32, (1, rows, wide), 2) & (rows - 1)
        diagonal = here == there
        mine = weights_ref[...].reshape(per_band * members, members)
        fields = arrived_ref[...].reshape(wide, arrived_ref.shape[-1])
        total = None
        sub = lax.broadcasted_iota(jnp.int32, (1, rows, wide), 1)
        for part in split(mine):
            tall = dot(part, spread)
            full = None
            for t in range(per_band):
                piece = tall[t * members : (t + 1) * members].reshape(members, 1, wide)
                own = diagonal & (sub >= t * tile_rows) & (sub < (t + 1) * tile_rows)
                full = jnp.where(own, piece, 0.0 if full is None else full)
            full = full.reshape(wide, wide).astype(jnp.bfloat16)
            term = dot(full, fields)
            total = term if total is None else total + term
        where = pl.ds(pl.multiple_of(step * rows, rows), rows)
        held[:, where, :] = total.reshape(members, rows, fields.shape[-1])

    @pl.when(step >= bands)
    def _():
        count, channels, strip, lat = out_ref.shape
        for k in range(count):
            j = (step - bands) * count + k
            out_ref[k] = held[j].T.reshape(channels, strip, lat)


def iterate(window, neighbours_ref, localization_ref, current, inverse, weights_ref):
    tiles, members = weights_ref.shape[:2]
    row = lax.broadcasted_iota(jnp.int32, (members, members), 0)
    col = lax.broadcasted_iota(jnp.int32, (members, members), 1)
    identity = jnp.where(row == col, 1.0, 0.0)

    def exact(a, b, dims=((1,), (0,))):
        return lax.dot_general(
            a, b, (dims, ((), ())),
            precision=lax.Precision.HIGHEST, preferred_element_type=jnp.float32,
        )

    def product(a, b):
        a_hi, a_lo = split(a)
        b_hi, b_lo = split(b)
        return dot(
            jnp.concatenate([a_hi, a_hi, a_lo], axis=1),
            jnp.concatenate([b_hi, b_lo, b_hi], axis=0),
        )

    scales, drives = [], []
    for t in range(tiles):
        total = None
        for n in range(neighbours_ref.shape[1]):
            term = localization_ref[t, n] * window[neighbours_ref[t, n]]
            total = term if total is None else total + term
        curvature = (members - 1.0) * identity + total[:members]
        scale = jnp.sqrt(jnp.sum(curvature * curvature, keepdims=True))
        scales.append(scale)
        drives.append(total[members:])
        current[t] = curvature / scale
        inverse[t] = identity

    def one(_, carry):
        for t in range(tiles):
            now, inv = current[t], inverse[t]
            middle = 1.5 * identity - 0.5 * product(inv, now)
            current[t] = product(now, middle)
            inverse[t] = product(middle, inv)
        return carry

    lax.fori_loop(0, NS_ITERS, one, 0)
    for t in range(tiles):
        inv = inverse[t]
        half = exact(drives[t], inv, ((1,), (1,)))
        shift = exact(half, inv, ((1,), (1,))) / scales[t]
        turned = jnp.sqrt((members - 1.0) / scales[t]) * inv.T + shift[0:1]
        weights_ref[t] = 1.0 / members + turned - jnp.mean(turned, axis=1, keepdims=True)


def transport_kernel(
    prior_ref, zonal_ref, north_ref, south_c_ref, below_ref, above_ref, gram_ref,
    neighbours_ref, localization_ref, got_ref, weights_ref,
    sent, window, current, inverse,
    own_sem, gram_own_sem, send_sems, recv_sems, gram_send_sems, gram_recv_sems,
):
    step, steps = pl.program_id(0), pl.num_programs(0)
    lat_count = lax.axis_size("lat")
    count = lax.axis_size("mem") * lat_count
    me = lax.axis_index("mem") * lat_count + lax.axis_index("lat")
    tiles = gram_ref.shape[0]
    chunks = send_sems.shape[0]
    per_chunk = steps // chunks
    chunk_rows = sent.shape[1] // chunks
    barrier = pltpu.get_barrier_semaphore()

    def place(d):
        return {"mem": d // lat_count, "lat": d % lat_count}

    def sending(chunk, k):
        to = (me + k) % count
        rows = pl.ds(pl.multiple_of(chunk * chunk_rows, chunk_rows), chunk_rows)
        return pltpu.make_async_remote_copy(
            src_ref=sent.at[to, rows],
            dst_ref=got_ref.at[me, rows],
            send_sem=send_sems.at[chunk, k],
            recv_sem=recv_sems.at[chunk, k],
            device_id=place(to),
            device_id_type=pl.DeviceIdType.MESH,
        )

    def arriving(chunk, k):
        origin = (me - k + count) % count
        rows = pl.ds(pl.multiple_of(chunk * chunk_rows, chunk_rows), chunk_rows)
        return pltpu.make_async_remote_copy(
            src_ref=sent.at[origin, rows],
            dst_ref=got_ref.at[origin, rows],
            send_sem=send_sems.at[chunk, k],
            recv_sem=recv_sems.at[chunk, k],
            device_id=place(origin),
            device_id_type=pl.DeviceIdType.MESH,
        )

    def gram_copy(side):
        to = (me + 1) % count if side == 0 else (me - 1 + count) % count
        return pltpu.make_async_remote_copy(
            src_ref=gram_ref,
            dst_ref=window.at[pl.ds(2 * tiles * side, tiles)],
            send_sem=gram_send_sems.at[side],
            recv_sem=gram_recv_sems.at[side],
            device_id=place(to),
            device_id_type=pl.DeviceIdType.MESH,
        )

    gram_own = pltpu.make_async_copy(gram_ref, window.at[pl.ds(tiles, tiles)], gram_own_sem)
    own = pltpu.make_async_copy(sent.at[me], got_ref.at[me], own_sem)

    @pl.when(step == 0)
    def _():
        def greet(k, carry):
            pl.semaphore_signal(
                barrier, inc=1, device_id=place((me + k) % count),
                device_id_type=pl.DeviceIdType.MESH,
            )
            return carry

        lax.fori_loop(1, count, greet, 0)
        pl.semaphore_wait(barrier, count - 1)
        gram_copy(0).start()
        gram_copy(1).start()
        gram_own.start()

    advance(
        prior_ref, zonal_ref, north_ref, south_c_ref, below_ref, above_ref, sent, step
    )

    @pl.when(step % per_chunk == per_chunk - 1)
    def _():
        def begin(k, carry):
            sending(step // per_chunk, k).start()
            return carry

        lax.fori_loop(1, count, begin, 0)

    @pl.when(step == steps - 1)
    def _():
        own.start()
        gram_own.wait()
        gram_copy(0).wait()
        gram_copy(1).wait()
        iterate(window, neighbours_ref, localization_ref, current, inverse, weights_ref)

        def finish(i, carry):
            chunk, k = i // (count - 1), i % (count - 1) + 1
            sending(chunk, k).wait_send()
            arriving(chunk, k).wait_recv()
            return carry

        lax.fori_loop(0, chunks * (count - 1), finish, 0)
        own.wait()


def shifted(axis, wrap):
    size = lax.axis_size(axis)
    up = [(i, (i + 1) % size) for i in range(size if wrap else size - 1)]
    down = [(j, i) for i, j in up]
    return up, down


def fast_device(
    prior_member_stack,
    zonal_stability_ratio,
    meridional_stability_ratio,
    obs_perturb,
    innovation,
    inverse_error_variance,
    obs_count,
    neighbours,
    localization,
):
    members_dev, channels, row_count, lon_count = prior_member_stack.shape
    mem_count = lax.axis_size("mem")
    lat_count = lax.axis_size("lat")
    devices = mem_count * lat_count
    strip = lon_count // devices
    members = members_dev * mem_count
    lat_total = row_count * lat_count
    tiles, slots = innovation.shape
    tile_rows = lat_total // tiles
    params = pltpu.CompilerParams(vmem_limit_bytes=VMEM_BYTES)

    up, down = shifted("lat", False)
    halo = members_dev * channels
    edges = (
        jnp.concatenate(
            [
                prior_member_stack[:, :, row_count - 1, :].reshape(halo, lon_count),
                jnp.broadcast_to(meridional_stability_ratio[row_count - 1 :], (8, lon_count)),
            ]
        ),
        prior_member_stack[:, :, 0, :].reshape(halo, lon_count),
    )
    *edges, obs_count = lax.optimization_barrier((*edges, obs_count))
    below = lax.ppermute(edges[0], "lat", up)
    above = lax.ppermute(edges[1], "lat", down)

    gram = pl.pallas_call(
        gram_kernel,
        grid=(tiles,),
        out_shape=jax.ShapeDtypeStruct((tiles, members + 8, members), jnp.float32),
        in_specs=[
            pl.BlockSpec((1, members, slots), lambda t: (t, 0, 0)),
            pl.BlockSpec((tiles, slots), lambda t: (0, 0)),
            pl.BlockSpec((tiles, slots), lambda t: (0, 0)),
            pl.BlockSpec(memory_space=pltpu.SMEM),
        ],
        out_specs=pl.BlockSpec((1, members + 8, members), lambda t: (t, 0, 0)),
        compiler_params=params,
        cost_estimate=pl.CostEstimate(
            flops=4 * obs_perturb.size * members, bytes_accessed=4 * obs_perturb.size, transcendentals=0
        ),
        name="gram",
    )(obs_perturb, innovation, inverse_error_variance, obs_count)

    pair, chunks = 2, 8
    wire = (devices, members_dev * row_count, channels * strip)
    square = (tiles, members, members)
    arrived, folded = pl.pallas_call(
        transport_kernel,
        grid=(members_dev // pair,),
        out_shape=(
            jax.ShapeDtypeStruct(wire, jnp.bfloat16),
            jax.ShapeDtypeStruct(square, jnp.float32),
        ),
        in_specs=[
            pl.BlockSpec((pair, channels, row_count, lon_count), lambda g: (g, 0, 0, 0)),
            pl.BlockSpec((row_count, lon_count), lambda g: (0, 0)),
            pl.BlockSpec((row_count, lon_count), lambda g: (0, 0)),
            pl.BlockSpec((8, lon_count), lambda g: (halo // 8, 0)),
            pl.BlockSpec((pair * channels, lon_count), lambda g: (g, 0)),
            pl.BlockSpec((pair * channels, lon_count), lambda g: (g, 0)),
            pl.BlockSpec(memory_space=pltpu.VMEM),
            pl.BlockSpec(memory_space=pltpu.SMEM),
            pl.BlockSpec(memory_space=pltpu.SMEM),
        ],
        out_specs=(
            pl.BlockSpec(memory_space=pl.ANY),
            pl.BlockSpec(square, lambda g: (0, 0, 0)),
        ),
        scratch_shapes=[
            pltpu.VMEM(wire, jnp.bfloat16),
            pltpu.VMEM((3 * tiles, members + 8, members), jnp.float32),
            pltpu.VMEM(square, jnp.float32),
            pltpu.VMEM(square, jnp.float32),
            pltpu.SemaphoreType.DMA(()),
            pltpu.SemaphoreType.DMA(()),
            pltpu.SemaphoreType.DMA((chunks, devices)),
            pltpu.SemaphoreType.DMA((chunks, devices)),
            pltpu.SemaphoreType.DMA((2,)),
            pltpu.SemaphoreType.DMA((2,)),
        ],
        compiler_params=pltpu.CompilerParams(
            collective_id=0, has_side_effects=True, vmem_limit_bytes=VMEM_BYTES
        ),
        name="transport",
    )(
        prior_member_stack,
        zonal_stability_ratio,
        meridional_stability_ratio,
        below,
        below,
        above,
        gram,
        neighbours,
        localization,
    )

    per_band = row_count // tile_rows
    j_block = 8
    j_steps = members // j_block
    last = lat_count - 1
    return pl.pallas_call(
        lambda *refs: analysis_kernel(lat_count, row_count, tile_rows, *refs),
        grid=(lat_count + j_steps,),
        out_shape=jax.ShapeDtypeStruct((members, channels, strip, lat_total), jnp.float32),
        in_specs=[
            pl.BlockSpec((per_band, members, members), lambda s: (jnp.minimum(s, last), 0, 0)),
            pl.BlockSpec(
                (mem_count, 1, members_dev * row_count, channels * strip),
                lambda s: (0, jnp.minimum(s, last), 0, 0),
            ),
        ],
        out_specs=pl.BlockSpec(
            (j_block, channels, strip, lat_total),
            lambda s: (jnp.maximum(s - lat_count, 0), 0, 0, 0),
        ),
        scratch_shapes=[pltpu.VMEM((members, lat_total, channels * strip), jnp.float32)],
        compiler_params=params,
        name="analysis",
    )(folded, arrived.reshape(mem_count, lat_count, members_dev * row_count, channels * strip))


def per_device(prior_member_stack, *rest):
    members_dev, channels, row_count, lon_count = prior_member_stack.shape
    lat_count = lax.axis_size("lat")
    devices = lax.axis_size("mem") * lat_count
    tiles = rest[3].shape[0]
    tile_rows = row_count * lat_count // tiles
    fits = (
        lon_count == 16 * devices
        and channels % 8 == 0
        and row_count == 8
        and tile_rows in (1, 2, 4, 8)
        and members_dev % 8 == 0
    )
    return (fast_device if fits else general_device)(prior_member_stack, *rest)


def solution(mesh):
    in_specs = (
        P("mem", None, "lat", None),
        P("lat", None),
        P("lat", None),
        P(("mem", "lat"), None, None),
        P(("mem", "lat"), None),
        P(("mem", "lat"), None),
        P(("mem", "lat")),
        P(("mem", "lat"), None),
        P(("mem", "lat"), None),
    )
    out_specs = P(None, None, ("mem", "lat"), None)
    return jax.shard_map(
        per_device, mesh=mesh, in_specs=in_specs, out_specs=out_specs, check_vma=False
    )
```
